32 devices in a mesh: dp: 4 (over z), ctx: 8 (over y, x, core).
Axes of the slice: x: 2, y: 2, z: 4, core: 2. Of those that a mesh axis runs over, the one named last changes fastest.
Arguments:
- inputs: bfloat16 [4, 1024, 3072], P('dp', 'ctx'), may hold values from -0.125 to 0.125
- queries: bfloat16 [4, 1024, 4096], P('dp', 'ctx'), may hold values from -0.875 to 0.875
- keys: bfloat16 [4, 1024, 4096], P('dp', 'ctx'), may hold values from -0.875 to 0.875
- values: bfloat16 [4, 1024, 4096], P('dp', 'ctx'), may hold values from -0.875 to 0.875
- out_grad: bfloat16 [4, 1024, 4096], P('dp', 'ctx'), may hold values from -0.875 to 0.875
- log_gate: float32 [4, 32, 1024], P('dp', None, 'ctx'), may hold values from -1 to 0
- boundaries: int32 [4, 4], P('dp'), may hold values from 1 to 1023, as said below
Outputs:
- query_grad: bfloat16 [4, 1024, 4096], P('dp', 'ctx')
- key_grad: bfloat16 [4, 1024, 4096], P('dp', 'ctx')
- value_weight_grad: float32 [3072, 4096], P('ctx', 'dp')
The draws below stay inside these ranges and needn't reach their ends.
Inputs may be any that keep to these rules, and one draw needn't show every extreme that they name: `boundaries`: boundary j of a sequence (counting from 0) lies between j * 256 + 1 and j * 256 + 255.
All inputs are finite; a program needn't handle non-finite values.
Results may differ from the reference program's by a relative error of at most 0.034.
Values may be sent and summed in bfloat16 or wider, within the bound.
A program may use at most 192 MiB of HBM per device.

```python
import jax
import jax.numpy as jnp
from jax import lax

HEADS = 32
HEAD = 128
DIM = 3072
TOK_DEV = 128
BOUNDS = 4
SEQUENCE_LENGTH = 1024
SEQUENCE_COUNT = 4
SEGMENT = 256
N_CTX = 8


def draw_log_gate(key, part):
    key = jax.random.fold_in(key, 7)
    random_subkeys = jax.random.split(key, 7)
    blocks = SEQUENCE_LENGTH // TOK_DEV
    head_shape = (SEQUENCE_COUNT, HEADS, 1)
    fast_share = 0.5
    quick_decay = jax.random.uniform(random_subkeys[0], head_shape) < fast_share
    fast_rate = jnp.exp(jax.random.uniform(random_subkeys[1], head_shape, minval=jnp.log(1.0 / 50.0), maxval=jnp.log(1.0 / 30.0)))
    slow_rate = jnp.exp(jax.random.uniform(random_subkeys[2], head_shape, minval=jnp.log(0.05), maxval=jnp.log(0.5))) / SEQUENCE_LENGTH
    baseline_decay_rate = jnp.where(quick_decay, fast_rate, slow_rate)
    block_factor = jnp.exp(jax.random.uniform(random_subkeys[3], (SEQUENCE_COUNT, HEADS, blocks), minval=jnp.log(0.5), maxval=jnp.log(2.0)))
    step_factor = jnp.exp(jax.random.uniform(random_subkeys[4], (SEQUENCE_COUNT, HEADS, SEQUENCE_LENGTH), minval=jnp.log(0.5), maxval=jnp.log(2.0)))
    decay_multiplier = jnp.repeat(block_factor, TOK_DEV, axis=2) * step_factor
    reset_position = jax.random.randint(random_subkeys[5], (SEQUENCE_COUNT, 1, 1, 3), 0, SEQUENCE_LENGTH)
    reset_locations = jnp.arange(SEQUENCE_LENGTH, dtype=jnp.int32)[None, None, :, None]
    reset_flags = jnp.minimum(jnp.sum((reset_locations == reset_position).astype(jnp.float32), axis=3), 1.0)
    loss_fraction = jax.random.uniform(random_subkeys[6], (SEQUENCE_COUNT, HEADS, SEQUENCE_LENGTH), minval=0.2, maxval=0.4)
    reset_event = jnp.where(quick_decay, 0.0, reset_flags * jnp.log(1.0 - loss_fraction))
    return (-baseline_decay_rate * decay_multiplier + reset_event).astype(jnp.float32)


def draw_boundaries(key, part):
    key = jax.random.fold_in(key, 3)
    offsets = jax.random.randint(key, (SEQUENCE_COUNT, BOUNDS), 1, SEGMENT)
    starts = jnp.arange(BOUNDS, dtype=jnp.int32) * SEGMENT
    return (starts[None, :] + offsets).astype(jnp.int32)


def raised(values, stream_key, source, target, blocks, factor):
    owner, partner = [(jnp.arange(values.shape[position]) // (values.shape[position] // blocks)).reshape([-1 if axis == position else 1 for axis in range(values.ndim)]) for position in (source, target)]
    chosen = jax.random.permutation(stream_key, blocks)[partner]
    strong = (owner == chosen) | (owner == (partner + blocks // 2) % blocks)
    return jnp.where(strong, factor * values, values)


def block_levels(key, extent, cuts, low, largest):
    gain, own = 1.0, jax.random.fold_in(key, 6)
    for position, shards_of in cuts:
        steps = jnp.exp(jax.random.uniform(jax.random.fold_in(own, position), (shards_of,), jnp.float32, low / len(cuts), largest / len(cuts)))
        gain = gain * jnp.repeat(steps, extent[position] // shards_of).reshape([-1 if axis == position else 1 for axis in range(len(extent))])
    return gain


def scatter_about(rng, extent, spread, reach, shards=(), held_as=jnp.bfloat16):
    values = spread * jax.random.normal(rng, extent, jnp.float32)
    if shards:
        values = values * block_levels(rng, extent, shards, -0.22, 0.18)
    return jnp.clip(values, -reach, reach).astype(held_as)


def bell_draw_with(rng, extent, spread, bound, cuts, heavy, held_as=jnp.bfloat16):
    values = spread * jax.random.normal(rng, extent, jnp.float32)
    if cuts:
        values = values * block_levels(rng, extent, cuts, -0.22, 0.18)
    return jnp.clip(raised(values, jax.random.fold_in(rng, 3), *heavy), -bound, bound).astype(held_as)


def setup_inputs(seed: int = 0) -> dict:
    key_of = jax.random.split(jax.random.key(seed), 8)
    inputs = bell_draw_with(key_of[0], (SEQUENCE_COUNT, SEQUENCE_LENGTH, DIM), ((SEQUENCE_COUNT * SEQUENCE_LENGTH) ** -0.5), 0.125, ((0, 4), (1, 8)), (1, 2, 8, 2.0))
    queries = scatter_about(key_of[1], (SEQUENCE_COUNT, SEQUENCE_LENGTH, HEADS * HEAD), ((HEAD * SEQUENCE_LENGTH) ** (-1.0 / 6)), 0.875, ((0, 4), (1, 8)))
    keys = scatter_about(key_of[2], (SEQUENCE_COUNT, SEQUENCE_LENGTH, HEADS * HEAD), ((HEAD * SEQUENCE_LENGTH) ** (-1.0 / 6)), 0.875, ((0, 4), (1, 8)))
    values = scatter_about(key_of[3], (SEQUENCE_COUNT, SEQUENCE_LENGTH, HEADS * HEAD), ((HEAD * SEQUENCE_LENGTH) ** (-1.0 / 6)), 0.875, ((0, 4), (1, 8)))
    out_grad = scatter_about(key_of[4], (SEQUENCE_COUNT, SEQUENCE_LENGTH, HEADS * HEAD), ((HEAD * SEQUENCE_LENGTH) ** (-1.0 / 6)), 0.875, ((0, 4), (1, 8)))
    log_gate = draw_log_gate(jax.random.fold_in(key_of[7], 71), 0)
    boundaries = draw_boundaries(jax.random.fold_in(key_of[7], 71), 0)
    return dict(inputs=inputs, queries=queries, keys=keys, values=values, out_grad=out_grad, log_gate=log_gate, boundaries=boundaries)


def rounded(value):
    return lax.optimization_barrier(value.astype(jnp.bfloat16)).astype(jnp.float32)


def block_tables(log_decay, positions, bounds):
    segment_ids = jnp.sum((bounds[None, :] <= positions[:, None]).astype(jnp.int32), axis=1)
    segment_in = jnp.sum((bounds <= positions[0] - 1).astype(jnp.int32))
    cumulative = jnp.cumsum(log_decay, axis=1)
    enter_weight = jnp.where((segment_ids == segment_in)[None, :], jnp.exp(cumulative), 0.0)
    leave_weight = jnp.where((segment_ids == segment_ids[-1])[None, :], jnp.exp(cumulative[:, -1:] - cumulative), 0.0)
    causal = (positions[:, None] >= positions[None, :]) & (segment_ids[:, None] == segment_ids[None, :])
    decay_table = jnp.exp(jnp.where(causal[None], cumulative[:, :, None] - cumulative[:, None, :], -1e30))
    return enter_weight, leave_weight, decay_table


def reference(inputs, queries, keys, values, out_grad, log_gate, boundaries):
    block_rows = TOK_DEV
    blocks = N_CTX
    feature_width = HEADS * HEAD

    def sequence_step(weight_total, member):
        tokens_in, query_seq, key_seq, value_seq, grad_seq, decay_seq, bounds = member

        def split_rows(array):
            return array.reshape(blocks, block_rows, HEADS, HEAD)

        query_blk = split_rows(query_seq)
        key_blk = split_rows(key_seq)
        value_blk = split_rows(value_seq)
        grad_blk = split_rows(grad_seq)
        token_blk = tokens_in.reshape(blocks, block_rows, DIM)
        decay_blk = decay_seq.reshape(HEADS, blocks, block_rows).transpose(1, 0, 2)
        block_ids = jnp.arange(blocks, dtype=jnp.int32)

        def local_states(item):
            block_id, log_decay, key_one, value_one, query_one, grad_one = item
            positions = block_id * block_rows + jnp.arange(block_rows, dtype=jnp.int32)
            enter_weight, leave_weight, decay_table = block_tables(log_decay, positions, bounds)
            weighted_keys = rounded(leave_weight.T[:, :, None] * key_one.astype(jnp.float32))
            local_state = jnp.einsum('shd,she->hde', weighted_keys, value_one.astype(jnp.float32))
            weighted_queries = rounded(enter_weight.T[:, :, None] * query_one.astype(jnp.float32))
            back_state = jnp.einsum('thd,the->hde', weighted_queries, grad_one.astype(jnp.float32))
            return enter_weight[:, -1], local_state, back_state

        through, local_state, back_state = lax.map(local_states, (block_ids, decay_blk, key_blk, value_blk, query_blk, grad_blk))

        def carry_step(state, item):
            decay_multiplier, term = item
            return rounded(decay_multiplier)[:, None, None] * state + rounded(term), rounded(state)

        zero_state = jnp.zeros((HEADS, HEAD, HEAD), jnp.float32)
        last_state, carried_in = lax.scan(carry_step, zero_state, (through, local_state))
        first_state, carried_back = lax.scan(carry_step, zero_state, (through, back_state), reverse=True)

        def gradient_step(weight_sum, item):
            block_id, log_decay, query_one, key_one, value_one, grad_one, token_one, state_in, state_back = item
            positions = block_id * block_rows + jnp.arange(block_rows, dtype=jnp.int32)
            enter_weight, leave_weight, decay_table = block_tables(log_decay, positions, bounds)
            query_f = query_one.astype(jnp.float32)
            key_f = key_one.astype(jnp.float32)
            value_f = value_one.astype(jnp.float32)
            grad_f = grad_one.astype(jnp.float32)
            score_grad = rounded(decay_table * jnp.einsum('thd,shd->hts', grad_f, value_f))
            score_keys = rounded(decay_table * jnp.einsum('thd,shd->hts', query_f, key_f))
            query_new = jnp.einsum('hts,shd->thd', score_grad, key_f) + enter_weight.T[:, :, None] * jnp.einsum('the,hde->thd', grad_f, state_in)
            key_new = jnp.einsum('hts,thd->shd', score_grad, query_f) + leave_weight.T[:, :, None] * jnp.einsum('she,hde->shd', value_f, state_back)
            value_new = jnp.einsum('hts,thd->shd', score_keys, grad_f) + leave_weight.T[:, :, None] * jnp.einsum('shd,hde->she', key_f, state_back)
            value_grad = value_new.astype(jnp.bfloat16).reshape(block_rows, feature_width)
            block_term = jnp.dot(token_one.T, value_grad, preferred_element_type=jnp.float32)
            weight_sum = weight_sum + rounded(block_term)
            return weight_sum, (query_new.astype(jnp.bfloat16).reshape(block_rows, feature_width), key_new.astype(jnp.bfloat16).reshape(block_rows, feature_width))

        weight_total, grads = lax.scan(gradient_step, weight_total, (block_ids, decay_blk, query_blk, key_blk, value_blk, grad_blk, token_blk, carried_in, carried_back))
        return weight_total, (grads[0].reshape(SEQUENCE_LENGTH, feature_width), grads[1].reshape(SEQUENCE_LENGTH, feature_width))

    weight_start = jnp.zeros((DIM, feature_width), jnp.float32)
    weight_total, grads = lax.scan(sequence_step, weight_start, (inputs, queries, keys, values, out_grad, log_gate, boundaries))
    return grads[0], grads[1], weight_total
```

```python
import jax
import jax.numpy as jnp
from jax import lax
from jax.sharding import PartitionSpec as P


def head_major(array, tok_rows, head_count, head_size):
    return array[0].reshape(tok_rows, head_count, head_size).transpose(1, 0, 2)


def row_major(array, tok_rows, feature_width):
    return array.astype(jnp.bfloat16).transpose(1, 0, 2).reshape(tok_rows, feature_width)


def per_device(inputs, queries, keys, values, out_grad, log_gate, boundaries):
    tok_rows = queries.shape[1]
    feature_width = queries.shape[2]
    head_count = log_gate.shape[1]
    head_size = feature_width // head_count
    query_one = head_major(queries, tok_rows, head_count, head_size)
    key_one = head_major(keys, tok_rows, head_count, head_size)
    value_one = head_major(values, tok_rows, head_count, head_size)
    grad_one = head_major(out_grad, tok_rows, head_count, head_size)
    token_one = inputs[0]
    bounds = boundaries[0]
    begin_at = lax.axis_index("ctx") * tok_rows
    positions = begin_at + jnp.arange(tok_rows, dtype=jnp.int32)
    segment_ids = jnp.sum((bounds[None, :] <= positions[:, None]).astype(jnp.int32), axis=1)
    segment_in = jnp.sum((bounds <= begin_at - 1).astype(jnp.int32))
    cumulative = jnp.cumsum(log_gate[0], axis=1)
    enter_weight = jnp.where((segment_ids == segment_in)[None, :], jnp.exp(cumulative), 0.0)
    leave_weight = jnp.where(
        (segment_ids == segment_ids[-1])[None, :], jnp.exp(cumulative[:, -1:] - cumulative), 0.0
    )
    causal = (positions[:, None] >= positions[None, :]) & (
        segment_ids[:, None] == segment_ids[None, :]
    )
    decay_table = jnp.exp(
        jnp.where(causal[None], cumulative[:, :, None] - cumulative[:, None, :], -1e30)
    )
    through = enter_weight[:, -1].astype(jnp.bfloat16)
    weighted_keys = (leave_weight[:, :, None] * key_one).astype(jnp.bfloat16)
    local_state = jnp.einsum(
        "hsd,hse->hde", weighted_keys, value_one, preferred_element_type=jnp.float32
    )
    weighted_queries = (enter_weight[:, :, None] * query_one).astype(jnp.bfloat16)
    back_state = jnp.einsum(
        "htd,hte->hde", weighted_queries, grad_one, preferred_element_type=jnp.float32
    )
    groups = lax.axis_size("ctx")
    extra = jnp.broadcast_to(through[:, None, None], (head_count, 16, head_size))
    packed = jnp.concatenate(
        [local_state.astype(jnp.bfloat16), back_state.astype(jnp.bfloat16), extra], axis=1
    )
    packed = lax.all_to_all(packed, "ctx", 0, 0, tiled=True)
    packed = packed.reshape(groups, head_count // groups, 2 * head_size + 16, head_size)
    ahead = packed[:, :, :head_size].astype(jnp.float32)
    behind = packed[:, :, head_size : 2 * head_size].astype(jnp.float32)
    factor = packed[:, :, 2 * head_size, :1, None].astype(jnp.float32)
    state_in = [jnp.zeros_like(ahead[0])]
    state_back = [jnp.zeros_like(ahead[0])]
    for block in range(groups - 1):
        state_in.append(factor[block] * state_in[-1] + ahead[block])
        late = groups - 1 - block
        state_back.append(factor[late] * state_back[-1] + behind[late])
    carried = jnp.concatenate([jnp.stack(state_in), jnp.stack(state_back[::-1])], axis=2)
    carried = carried.astype(jnp.bfloat16).reshape(head_count, 2 * head_size, head_size)
    carried = lax.all_to_all(carried, "ctx", 0, 0, tiled=True)
    carried_in, carried_back = carried[:, :head_size], carried[:, head_size:]
    score_grad = (
        decay_table
        * jnp.einsum("htd,hsd->hts", grad_one, value_one, preferred_element_type=jnp.float32)
    ).astype(jnp.bfloat16)
    score_keys = (
        decay_table
        * jnp.einsum("htd,hsd->hts", query_one, key_one, preferred_element_type=jnp.float32)
    ).astype(jnp.bfloat16)
    query_new = jnp.einsum(
        "hts,hsd->htd", score_grad, key_one, preferred_element_type=jnp.float32
    ) + enter_weight[:, :, None] * jnp.einsum(
        "hte,hde->htd", grad_one, carried_in, preferred_element_type=jnp.float32
    )
    key_new = jnp.einsum(
        "hts,htd->hsd", score_grad, query_one, preferred_element_type=jnp.float32
    ) + leave_weight[:, :, None] * jnp.einsum(
        "hse,hde->hsd", value_one, carried_back, preferred_element_type=jnp.float32
    )
    value_new = jnp.einsum(
        "hts,htd->hsd", score_keys, grad_one, preferred_element_type=jnp.float32
    ) + leave_weight[:, :, None] * jnp.einsum(
        "hsd,hde->hse", key_one, carried_back, preferred_element_type=jnp.float32
    )
    query_grad = row_major(query_new, tok_rows, feature_width).reshape(1, tok_rows, feature_width)
    key_grad = row_major(key_new, tok_rows, feature_width).reshape(1, tok_rows, feature_width)
    value_grad = row_major(value_new, tok_rows, feature_width)
    token_all = lax.all_to_all(token_one, "ctx", 1, 0, tiled=True)
    token_all = lax.all_gather(token_all, "dp")
    value_all = lax.all_to_all(value_grad, "dp", 1, 0, tiled=True)
    value_all = lax.all_gather(value_all, "ctx")
    sequences = token_all.shape[0]
    token_all = token_all.reshape(sequences, groups, tok_rows, -1).transpose(1, 0, 2, 3)
    token_all = token_all.reshape(groups * sequences * tok_rows, -1)
    value_all = value_all.reshape(groups * sequences * tok_rows, -1)
    weight_grad = lax.dot_general(
        token_all, value_all, (((0,), (0,)), ((), ())), preferred_element_type=jnp.float32
    )
    return (query_grad, key_grad, weight_grad)


def solution(mesh):
    in_specs = (
        P("dp", "ctx", None),
        P("dp", "ctx", None),
        P("dp", "ctx", None),
        P("dp", "ctx", None),
        P("dp", "ctx", None),
        P("dp", None, "ctx"),
        P("dp", None),
    )
    out_specs = (P("dp", "ctx", None), P("dp", "ctx", None), P("ctx", "dp"))
    return jax.shard_map(
        per_device, mesh=mesh, in_specs=in_specs, out_specs=out_specs, check_vma=False
    )
```

```python
import functools

import jax
import jax.numpy as jnp
from jax import lax
from jax.experimental import pallas as pl
from jax.experimental.pallas import tpu as pltpu
from jax.sharding import PartitionSpec as P


def head_major(array, tok_rows, head_count, head_size):
    return array[0].reshape(tok_rows, head_count, head_size).transpose(1, 0, 2)


def row_major(array, tok_rows, feature_width):
    return array.astype(jnp.bfloat16).transpose(1, 0, 2).reshape(tok_rows, feature_width)


def per_device_plain(inputs, queries, keys, values, out_grad, log_gate, boundaries):
    tok_rows = queries.shape[1]
    feature_width = queries.shape[2]
    head_count = log_gate.shape[1]
    head_size = feature_width // head_count
    query_one = head_major(queries, tok_rows, head_count, head_size)
    key_one = head_major(keys, tok_rows, head_count, head_size)
    value_one = head_major(values, tok_rows, head_count, head_size)
    grad_one = head_major(out_grad, tok_rows, head_count, head_size)
    token_one = inputs[0]
    bounds = boundaries[0]
    begin_at = lax.axis_index("ctx") * tok_rows
    positions = begin_at + jnp.arange(tok_rows, dtype=jnp.int32)
    segment_ids = jnp.sum((bounds[None, :] <= positions[:, None]).astype(jnp.int32), axis=1)
    segment_in = jnp.sum((bounds <= begin_at - 1).astype(jnp.int32))
    cumulative = jnp.cumsum(log_gate[0], axis=1)
    enter_weight = jnp.where((segment_ids == segment_in)[None, :], jnp.exp(cumulative), 0.0)
    leave_weight = jnp.where(
        (segment_ids == segment_ids[-1])[None, :], jnp.exp(cumulative[:, -1:] - cumulative), 0.0
    )
    causal = (positions[:, None] >= positions[None, :]) & (
        segment_ids[:, None] == segment_ids[None, :]
    )
    decay_table = jnp.exp(
        jnp.where(causal[None], cumulative[:, :, None] - cumulative[:, None, :], -1e30)
    )
    through = enter_weight[:, -1].astype(jnp.bfloat16)
    weighted_keys = (leave_weight[:, :, None] * key_one).astype(jnp.bfloat16)
    local_state = jnp.einsum(
        "hsd,hse->hde", weighted_keys, value_one, preferred_element_type=jnp.float32
    )
    weighted_queries = (enter_weight[:, :, None] * query_one).astype(jnp.bfloat16)
    back_state = jnp.einsum(
        "htd,hte->hde", weighted_queries, grad_one, preferred_element_type=jnp.float32
    )
    groups = lax.axis_size("ctx")
    extra = jnp.broadcast_to(through[:, None, None], (head_count, 16, head_size))
    packed = jnp.concatenate(
        [local_state.astype(jnp.bfloat16), back_state.astype(jnp.bfloat16), extra], axis=1
    )
    packed = lax.all_to_all(packed, "ctx", 0, 0, tiled=True)
    packed = packed.reshape(groups, head_count // groups, 2 * head_size + 16, head_size)
    ahead = packed[:, :, :head_size].astype(jnp.float32)
    behind = packed[:, :, head_size : 2 * head_size].astype(jnp.float32)
    factor = packed[:, :, 2 * head_size, :1, None].astype(jnp.float32)
    state_in = [jnp.zeros_like(ahead[0])]
    state_back = [jnp.zeros_like(ahead[0])]
    for block in range(groups - 1):
        state_in.append(factor[block] * state_in[-1] + ahead[block])
        late = groups - 1 - block
        state_back.append(factor[late] * state_back[-1] + behind[late])
    carried = jnp.concatenate([jnp.stack(state_in), jnp.stack(state_back[::-1])], axis=2)
    carried = carried.astype(jnp.bfloat16).reshape(head_count, 2 * head_size, head_size)
    carried = lax.all_to_all(carried, "ctx", 0, 0, tiled=True)
    carried_in, carried_back = carried[:, :head_size], carried[:, head_size:]
    score_grad = (
        decay_table
        * jnp.einsum("htd,hsd->hts", grad_one, value_one, preferred_element_type=jnp.float32)
    ).astype(jnp.bfloat16)
    score_keys = (
        decay_table
        * jnp.einsum("htd,hsd->hts", query_one, key_one, preferred_element_type=jnp.float32)
    ).astype(jnp.bfloat16)
    query_new = jnp.einsum(
        "hts,hsd->htd", score_grad, key_one, preferred_element_type=jnp.float32
    ) + enter_weight[:, :, None] * jnp.einsum(
        "hte,hde->htd", grad_one, carried_in, preferred_element_type=jnp.float32
    )
    key_new = jnp.einsum(
        "hts,htd->hsd", score_grad, query_one, preferred_element_type=jnp.float32
    ) + leave_weight[:, :, None] * jnp.einsum(
        "hse,hde->hsd", value_one, carried_back, preferred_element_type=jnp.float32
    )
    value_new = jnp.einsum(
        "hts,htd->hsd", score_keys, grad_one, preferred_element_type=jnp.float32
    ) + leave_weight[:, :, None] * jnp.einsum(
        "hsd,hde->hse", key_one, carried_back, preferred_element_type=jnp.float32
    )
    query_grad = row_major(query_new, tok_rows, feature_width).reshape(1, tok_rows, feature_width)
    key_grad = row_major(key_new, tok_rows, feature_width).reshape(1, tok_rows, feature_width)
    value_grad = row_major(value_new, tok_rows, feature_width)
    token_all = lax.all_to_all(token_one, "ctx", 1, 0, tiled=True)
    token_all = lax.all_gather(token_all, "dp")
    value_all = lax.all_to_all(value_grad, "dp", 1, 0, tiled=True)
    value_all = lax.all_gather(value_all, "ctx")
    sequences = token_all.shape[0]
    token_all = token_all.reshape(sequences, groups, tok_rows, -1).transpose(1, 0, 2, 3)
    token_all = token_all.reshape(groups * sequences * tok_rows, -1)
    value_all = value_all.reshape(groups * sequences * tok_rows, -1)
    weight_grad = lax.dot_general(
        token_all, value_all, (((0,), (0,)), ((), ())), preferred_element_type=jnp.float32
    )
    return (query_grad, key_grad, weight_grad)


F32, BF16 = jnp.float32, jnp.bfloat16


def dot(left, right, left_dim, right_dim):
    return lax.dot_general(
        left, right, (((left_dim,), (right_dim,)), ((), ())), preferred_element_type=F32
    )


def push(src, dst, send_sem, recv_sem, dp, ctx):
    return pltpu.make_async_remote_copy(
        src_ref=src,
        dst_ref=dst,
        send_sem=send_sem,
        recv_sem=recv_sem,
        device_id=(dp, ctx),
        device_id_type=pl.DeviceIdType.MESH,
    )


def fused(
    planes, blocks, q, k, v, g, x, gate, bounds, qg, kg, wg,
    cum, decay_bias, enter_bias, leave_bias, through, xt_own, xt,
    local, mate_local, chip_state, arrived, carried, mate_carried, qi, ki, vi, vsend, vall,
    t_s, t_r, xa_s, xa_r, xz_s, xz_r, m1_s, m1_r, cs_s, cs_r, m2_s, m2_r, vz_s, vz_r,
    vb_s, vb_r, vm_s, vm_r,
):
    tok, feature = q.shape
    heads = gate.shape[0]
    size = feature // heads
    chunk = heads // planes
    half = chunk // 2
    rows = xt.shape[1]
    chips = blocks // 2
    d, c = lax.axis_index("dp"), lax.axis_index("ctx")
    core, chip = lax.rem(c, 2), lax.div(c, 2)
    mate = c + 1 - 2 * core
    first = core == 0

    barrier = pltpu.get_barrier_semaphore()
    for step in range(1, blocks):
        pl.semaphore_signal(
            barrier, inc=1, device_id=(d, lax.rem(c + step, blocks)),
            device_id_type=pl.DeviceIdType.MESH,
        )
    for step in range(1, planes):
        pl.semaphore_signal(
            barrier, inc=1, device_id=(lax.rem(d + step, planes), c),
            device_id_type=pl.DeviceIdType.MESH,
        )

    for part in range(x.shape[1] // 128):
        xt_own[part * 128 : (part + 1) * 128, :] = x[:, part * 128 : (part + 1) * 128].T
    pl.semaphore_wait(barrier, blocks - 1 + planes - 1)

    def columns(block):
        return pl.ds(pl.multiple_of(block * tok, tok), tok)

    def token_push(step):
        to = lax.rem(c + step, blocks)
        return push(
            xt_own.at[pl.ds(pl.multiple_of(to * rows, rows), rows), :],
            xt.at[d, :, columns(c)], xa_s.at[step - 1], xa_r.at[step - 1], d, to,
        )

    for step in range(1, blocks):
        token_push(step).start()
    xt[d, :, columns(c)] = xt_own[pl.ds(pl.multiple_of(c * rows, rows), rows), :]

    begin = c * tok
    at_t = lax.broadcasted_iota(jnp.int32, (tok, tok), 0)
    at_s = lax.broadcasted_iota(jnp.int32, (tok, tok), 1)
    seg_t = jnp.zeros((tok, tok), jnp.int32)
    seg_s = jnp.zeros((tok, tok), jnp.int32)
    seg_in = jnp.zeros((tok, tok), jnp.int32)
    seg_last = jnp.zeros((tok, tok), jnp.int32)
    for index in range(bounds.shape[1]):
        edge = jnp.full((tok, tok), bounds[0, index] - begin, jnp.int32)
        seg_t += (edge <= at_t).astype(jnp.int32)
        seg_s += (edge <= at_s).astype(jnp.int32)
        seg_in += (edge <= -1).astype(jnp.int32)
        seg_last += (edge <= tok - 1).astype(jnp.int32)
    decay_bias[...] = jnp.where((at_t >= at_s) & (seg_t == seg_s), 0.0, -1e30)
    enter_bias[...] = jnp.where(seg_t == seg_in, 0.0, -1e30)
    leave_bias[...] = jnp.where(seg_t == seg_last, 0.0, -1e30)
    cum[...] = lax.dot_general(
        gate[...], (at_t <= at_s).astype(F32), (((1,), (0,)), ((), ())),
        precision=lax.Precision.HIGHEST, preferred_element_type=F32,
    )
    total = jnp.broadcast_to(cum[:, tok - 1 : tok], (heads, size))
    through[c] = jnp.exp(total + enter_bias[tok - 1 : tok, :]).astype(BF16).astype(F32)

    def through_push(step):
        return push(
            through.at[c], through.at[c], t_s.at[step - 1], t_r.at[step - 1],
            d, lax.rem(c + step, blocks),
        )

    for step in range(1, blocks):
        through_push(step).start()

    def head_columns(head):
        return pl.ds(pl.multiple_of(head * size, size), size)

    def weights(head):
        at_row = jnp.broadcast_to(cum[pl.ds(head, 1), :], (size, tok))
        at_col = at_row.T
        enter = jnp.exp(at_col + enter_bias[...])
        leave = jnp.exp(at_col[tok - 1 : tok, :] - at_col + leave_bias[...])
        return at_row, at_col, enter, leave

    def chunk_head(i, j):
        return lax.rem(d + i, planes) * chunk + j

    def mate_push(i):
        return push(local.at[i, 1 - core], mate_local.at[i], m1_s.at[i], m1_r.at[i], d, mate)

    def local_chunk(i, carry):
        for j in range(chunk):
            head = chunk_head(i, j)
            cols = head_columns(head)
            _, _, enter, leave = weights(head)
            weighted_keys = (leave * k[:, cols].astype(F32)).astype(BF16)
            weighted_queries = (enter * q[:, cols].astype(F32)).astype(BF16)
            local[i, j // half, 0, j % half] = dot(weighted_keys, v[:, cols], 0, 0).astype(BF16)
            local[i, j // half, 1, j % half] = dot(weighted_queries, g[:, cols], 0, 0).astype(BF16)
        mate_push(i).start()
        return carry

    lax.fori_loop(0, planes, local_chunk, 0)

    for step in range(1, blocks):
        frm = lax.rem(c - step + blocks, blocks)
        push(
            through.at[frm], through.at[frm], t_s.at[step - 1], t_r.at[step - 1], d, frm
        ).wait_recv()

    def state_push(i, step):
        ahead = chip + step
        return push(
            chip_state.at[i, lax.div(ahead, chips)], arrived.at[i, step - 1],
            cs_s.at[i, step - 1], cs_r.at[i, step - 1], d, 2 * lax.rem(ahead, chips) + core,
        )

    def chip_chunk(i, carry):
        mate_push(i).wait_recv()
        for j in range(half):
            head = chunk_head(i, core * half + j)
            mine = through[c, pl.ds(head, 1), :]
            other = through[mate, pl.ds(head, 1), :]
            chip_state[i, 0, j] = (
                jnp.where(first, other, 1.0) * local[i, core, 0, j].astype(F32)
                + jnp.where(first, 1.0, mine) * mate_local[i, 0, j].astype(F32)
            ).astype(BF16)
            chip_state[i, 1, j] = (
                jnp.where(first, 1.0, other) * local[i, core, 1, j].astype(F32)
                + jnp.where(first, mine, 1.0) * mate_local[i, 1, j].astype(F32)
            ).astype(BF16)
        for step in range(1, chips):
            state_push(i, step).start()
        return carry

    lax.fori_loop(0, planes, chip_chunk, 0)

    for step in range(1, blocks):
        token_push(step).wait_send()
        frm = lax.rem(c - step + blocks, blocks)
        push(
            xt.at[d, :, columns(frm)], xt.at[d, :, columns(frm)],
            xa_s.at[step - 1], xa_r.at[step - 1], d, frm,
        ).wait_recv()

    def chain(step, act):
        @pl.when((d >= step - 1) & (d + 1 < planes))
        def _():
            piece = xt.at[d - (step - 1)]
            act(push(piece, piece, xz_s.at[0, step - 1], xz_r.at[0, step - 1], d + 1, c))

        @pl.when((d + step - 1 < planes) & (d >= 1))
        def _():
            piece = xt.at[d + step - 1]
            act(push(piece, piece, xz_s.at[1, step - 1], xz_r.at[1, step - 1], d - 1, c))

    def chain_wait(step):
        @pl.when(d >= step)
        def _():
            piece = xt.at[d - step]
            push(piece, piece, xz_s.at[0, step - 1], xz_r.at[0, step - 1], d - 1, c).wait_recv()

        @pl.when(d + step < planes)
        def _():
            piece = xt.at[d + step]
            push(piece, piece, xz_s.at[1, step - 1], xz_r.at[1, step - 1], d + 1, c).wait_recv()

    chain(1, lambda copy: copy.start())

    group = 4

    def inner(index, carry):
        for j in range(group):
            head = index * group + j
            cols = head_columns(head)
            at_row = jnp.broadcast_to(cum[pl.ds(head, 1), :], (size, tok))
            decay = jnp.exp(at_row.T - at_row + decay_bias[...])
            qh, kh, vh, gh = q[:, cols], k[:, cols], v[:, cols], g[:, cols]
            score_grad = (decay * dot(gh, vh, 1, 1)).astype(BF16)
            score_keys = (decay * dot(qh, kh, 1, 1)).astype(BF16)
            qi[:, cols] = dot(score_grad, kh, 1, 0)
            ki[:, cols] = dot(score_grad, qh, 0, 0)
            vi[:, cols] = dot(score_keys, gh, 0, 0)
        return carry

    lax.fori_loop(0, heads // group, inner, 0)

    def carried_push(i):
        return push(mate_carried.at[i], carried.at[i, core], m2_s.at[i], m2_r.at[i], d, mate)

    def carry_chunk(i):
        for step in range(1, chips):
            state_push(i, step).wait_recv()
        for j in range(half):
            head = chunk_head(i, core * half + j)
            mine = through[c, pl.ds(head, 1), :]
            other = through[mate, pl.ds(head, 1), :]
            sums = []
            for back in (False, True):
                state = jnp.zeros((size, size), F32)
                weight = jnp.ones((1, size), F32)
                for far in range(1, chips):
                    if back:
                        valid = chip + far < chips
                        source, slot = lax.rem(chip + far, chips), chips - far - 1
                    else:
                        valid = chip >= far
                        source, slot = lax.rem(chip - far + chips, chips), far - 1
                    state += jnp.where(valid, weight, 0.0) * arrived[i, slot, j].astype(F32)
                    weight = weight * (
                        through[2 * source, pl.ds(head, 1), :]
                        * through[2 * source + 1, pl.ds(head, 1), :]
                    )
                sums.append(state)
            came, back = sums
            late = jnp.where(first, 0.0, 1.0)
            early = 1.0 - late
            carried[i, core, 0, j] = (
                jnp.where(first, 1.0, other) * came + late * mate_local[i, 0, j].astype(F32)
            ).astype(BF16)
            carried[i, core, 1, j] = (
                jnp.where(first, other, 1.0) * back + early * mate_local[i, 1, j].astype(F32)
            ).astype(BF16)
            mate_carried[i, 0, j] = (
                jnp.where(first, mine, 1.0) * came + early * local[i, core, 0, j].astype(F32)
            ).astype(BF16)
            mate_carried[i, 1, j] = (
                jnp.where(first, 1.0, mine) * back + late * local[i, core, 1, j].astype(F32)
            ).astype(BF16)
        carried_push(i).start()

    def value_push(i):
        return push(
            vsend.at[i], vall.at[d, c], vz_s.at[i], vz_r.at[i], lax.rem(d + i, planes), c
        )

    def finish(i):
        push(
            carried.at[i, 1 - core], carried.at[i, 1 - core], m2_s.at[i], m2_r.at[i], d, mate
        ).wait_recv()
        for j in range(chunk):
            head = chunk_head(i, j)
            cols = head_columns(head)
            _, _, enter, leave = weights(head)
            came = carried[i, j // half, 0, j % half]
            back = carried[i, j // half, 1, j % half]
            vsend[i, :, j * size : (j + 1) * size] = (
                vi[:, cols] + leave * dot(k[:, cols], back, 1, 0)
            ).astype(BF16)
            qg[:, cols] = (qi[:, cols] + enter * dot(g[:, cols], came, 1, 1)).astype(BF16)
            kg[:, cols] = (ki[:, cols] + leave * dot(v[:, cols], back, 1, 1)).astype(BF16)
        if i == 0:
            vall[d, c] = vsend[0]
        else:
            value_push(i).start()

    def source_plane(i):
        return lax.rem(d - i + planes, planes)

    def spread(i, act):
        piece = vall.at[source_plane(i), c]
        for step in range(1, chips):
            to = 2 * lax.rem(chip + step, chips) + core
            act(push(piece, piece, vb_s.at[i, step - 1], vb_r.at[i, step - 1], d, to))
        act(push(piece, piece, vm_s.at[i, 0], vm_r.at[i, 0], d, mate))

    def receive(i):
        if i:
            piece = vall.at[source_plane(i), c]
            push(piece, piece, vz_s.at[i], vz_r.at[i], source_plane(i), c).wait_recv()
        spread(i, lambda copy: copy.start())

    def forward(i, act, wait):
        for step in range(1, chips):
            frm = 2 * lax.rem(chip - step + chips, chips) + core
            piece = vall.at[source_plane(i), frm]
            if wait:
                push(
                    piece, piece, vb_s.at[i, step - 1], vb_r.at[i, step - 1], d, frm
                ).wait_recv()
            act(push(piece, piece, vm_s.at[i, step], vm_r.at[i, step], d, mate))

    def multiply(i):
        plane = source_plane(i)
        for step in range(chips):
            frm = 2 * lax.rem(chip - step + chips, chips) + 1 - core
            piece = vall.at[plane, frm]
            push(piece, piece, vm_s.at[i, step], vm_r.at[i, step], d, mate).wait_recv()
        width = 256

        def tile(index, carry):
            cols = pl.ds(pl.multiple_of(index * width, width), width)
            right = vall[plane, :, :, cols].reshape(blocks * tok, width)
            product = dot(xt[plane], right, 1, 0)
            wg[:, cols] = product if i == 0 else wg[:, cols] + product
            return carry

        lax.fori_loop(0, wg.shape[1] // width, tile, 0)

    start = lambda copy: copy.start()
    done = 1
    carry_chunk(0)
    for i in range(planes):
        if i + 1 < planes:
            carry_chunk(i + 1)
        finish(i)
        if i != 1:
            receive(max(i - 1, 0))
        if done < planes - 1 and i % 2 == 0:
            chain_wait(done)
            done += 1
            chain(done, start)
    forward(0, start, True)
    receive(planes - 1)
    while done < planes - 1:
        chain_wait(done)
        done += 1
        chain(done, start)
    for i in range(1, planes):
        forward(i, start, True)
        multiply(i - 1)
        if i == 1:
            chain_wait(done)
    multiply(planes - 1)

    for step in range(1, blocks):
        through_push(step).wait_send()
    for step in range(1, planes):
        chain(step, lambda copy: copy.wait_send())
    for i in range(planes):
        mate_push(i).wait_send()
        carried_push(i).wait_send()
        for step in range(1, chips):
            state_push(i, step).wait_send()
        if i:
            value_push(i).wait_send()
        spread(i, lambda copy: copy.wait_send())
        forward(i, lambda copy: copy.wait_send(), False)


def per_device_fused(planes, blocks, inputs, queries, keys, values, out_grad, log_gate, boundaries):
    tok, feature = queries.shape[1:]
    heads = log_gate.shape[1]
    size = feature // heads
    chunk = heads // planes
    half = chunk // 2
    chips = blocks // 2
    width = feature // planes
    rows = inputs.shape[2] // blocks
    vmem = pl.BlockSpec(memory_space=pltpu.VMEM)
    sem = pltpu.SemaphoreType.DMA
    scratch = [
        pltpu.VMEM((heads, tok), F32),
        pltpu.VMEM((tok, tok), F32),
        pltpu.VMEM((tok, tok), F32),
        pltpu.VMEM((tok, tok), F32),
        pltpu.VMEM((blocks, heads, size), F32),
        pltpu.VMEM((inputs.shape[2], tok), BF16),
        pltpu.VMEM((planes, rows, blocks * tok), BF16),
        pltpu.VMEM((planes, 2, 2, half, size, size), BF16),
        pltpu.VMEM((planes, 2, half, size, size), BF16),
        pltpu.VMEM((planes, 2, half, size, size), BF16),
        pltpu.VMEM((planes, chips - 1, half, size, size), BF16),
        pltpu.VMEM((planes, 2, 2, half, size, size), BF16),
        pltpu.VMEM((planes, 2, half, size, size), BF16),
        pltpu.VMEM((tok, feature), F32),
        pltpu.VMEM((tok, feature), F32),
        pltpu.VMEM((tok, feature), F32),
        pltpu.VMEM((planes, tok, width), BF16),
        pltpu.VMEM((planes, blocks, tok, width), BF16),
        sem((blocks - 1,)), sem((blocks - 1,)),
        sem((blocks - 1,)), sem((blocks - 1,)),
        sem((2, planes - 1)), sem((2, planes - 1)),
        sem((planes,)), sem((planes,)),
        sem((planes, chips - 1)), sem((planes, chips - 1)),
        sem((planes,)), sem((planes,)),
        sem((planes,)), sem((planes,)),
        sem((planes, chips - 1)), sem((planes, chips - 1)),
        sem((planes, chips)), sem((planes, chips)),
    ]
    query_grad, key_grad, weight_grad = pl.pallas_call(
        functools.partial(fused, planes, blocks),
        out_shape=(
            jax.ShapeDtypeStruct((tok, feature), BF16),
            jax.ShapeDtypeStruct((tok, feature), BF16),
            jax.ShapeDtypeStruct((rows, width), F32),
        ),
        in_specs=[vmem] * 6 + [pl.BlockSpec(memory_space=pltpu.SMEM)],
        out_specs=(vmem, vmem, vmem),
        scratch_shapes=scratch,
        compiler_params=pltpu.CompilerParams(
            collective_id=0, has_side_effects=True, vmem_limit_bytes=VMEM_LIMIT
        ),
    )(queries[0], keys[0], values[0], out_grad[0], inputs[0], log_gate[0], boundaries)
    return query_grad[None], key_grad[None], weight_grad


VMEM_LIMIT = 60 * 2**20


def per_device(mesh, inputs, queries, keys, values, out_grad, log_gate, boundaries):
    planes, blocks = mesh.shape["dp"], mesh.shape["ctx"]
    arrays = (inputs, queries, keys, values, out_grad, log_gate, boundaries)
    tok, feature = queries.shape[1:]
    gathered = 2 * planes * blocks * tok * (feature // planes + inputs.shape[2] // blocks)
    if gathered + 32 * tok * feature * 2 > VMEM_LIMIT:
        return per_device_plain(*arrays)
    return per_device_fused(planes, blocks, *arrays)


def solution(mesh):
    in_specs = (
        P("dp", "ctx", None),
        P("dp", "ctx", None),
        P("dp", "ctx", None),
        P("dp", "ctx", None),
        P("dp", "ctx", None),
        P("dp", None, "ctx"),
        P("dp", None),
    )
    out_specs = (P("dp", "ctx", None), P("dp", "ctx", None), P("ctx", "dp"))
    return jax.shard_map(
        functools.partial(per_device, mesh), mesh=mesh, in_specs=in_specs, out_specs=out_specs, check_vma=False
    )
```

```python
import functools

import jax
import jax.numpy as jnp
from jax import lax
from jax.experimental import pallas as pl
from jax.experimental.pallas import tpu as pltpu
from jax.sharding import PartitionSpec as P


def head_major(array, tok_rows, head_count, head_size):
    return array[0].reshape(tok_rows, head_count, head_size).transpose(1, 0, 2)


def row_major(array, tok_rows, feature_width):
    return array.astype(jnp.bfloat16).transpose(1, 0, 2).reshape(tok_rows, feature_width)


def per_device_plain(inputs, queries, keys, values, out_grad, log_gate, boundaries):
    tok_rows = queries.shape[1]
    feature_width = queries.shape[2]
    head_count = log_gate.shape[1]
    head_size = feature_width // head_count
    query_one = head_major(queries, tok_rows, head_count, head_size)
    key_one = head_major(keys, tok_rows, head_count, head_size)
    value_one = head_major(values, tok_rows, head_count, head_size)
    grad_one = head_major(out_grad, tok_rows, head_count, head_size)
    token_one = inputs[0]
    bounds = boundaries[0]
    begin_at = lax.axis_index("ctx") * tok_rows
    positions = begin_at + jnp.arange(tok_rows, dtype=jnp.int32)
    segment_ids = jnp.sum((bounds[None, :] <= positions[:, None]).astype(jnp.int32), axis=1)
    segment_in = jnp.sum((bounds <= begin_at - 1).astype(jnp.int32))
    cumulative = jnp.cumsum(log_gate[0], axis=1)
    enter_weight = jnp.where((segment_ids == segment_in)[None, :], jnp.exp(cumulative), 0.0)
    leave_weight = jnp.where(
        (segment_ids == segment_ids[-1])[None, :], jnp.exp(cumulative[:, -1:] - cumulative), 0.0
    )
    causal = (positions[:, None] >= positions[None, :]) & (
        segment_ids[:, None] == segment_ids[None, :]
    )
    decay_table = jnp.exp(
        jnp.where(causal[None], cumulative[:, :, None] - cumulative[:, None, :], -1e30)
    )
    through = enter_weight[:, -1].astype(jnp.bfloat16)
    weighted_keys = (leave_weight[:, :, None] * key_one).astype(jnp.bfloat16)
    local_state = jnp.einsum(
        "hsd,hse->hde", weighted_keys, value_one, preferred_element_type=jnp.float32
    )
    weighted_queries = (enter_weight[:, :, None] * query_one).astype(jnp.bfloat16)
    back_state = jnp.einsum(
        "htd,hte->hde", weighted_queries, grad_one, preferred_element_type=jnp.float32
    )
    groups = lax.axis_size("ctx")
    extra = jnp.broadcast_to(through[:, None, None], (head_count, 16, head_size))
    packed = jnp.concatenate(
        [local_state.astype(jnp.bfloat16), back_state.astype(jnp.bfloat16), extra], axis=1
    )
    packed = lax.all_to_all(packed, "ctx", 0, 0, tiled=True)
    packed = packed.reshape(groups, head_count // groups, 2 * head_size + 16, head_size)
    ahead = packed[:, :, :head_size].astype(jnp.float32)
    behind = packed[:, :, head_size : 2 * head_size].astype(jnp.float32)
    factor = packed[:, :, 2 * head_size, :1, None].astype(jnp.float32)
    state_in = [jnp.zeros_like(ahead[0])]
    state_back = [jnp.zeros_like(ahead[0])]
    for block in range(groups - 1):
        state_in.append(factor[block] * state_in[-1] + ahead[block])
        late = groups - 1 - block
        state_back.append(factor[late] * state_back[-1] + behind[late])
    carried = jnp.concatenate([jnp.stack(state_in), jnp.stack(state_back[::-1])], axis=2)
    carried = carried.astype(jnp.bfloat16).reshape(head_count, 2 * head_size, head_size)
    carried = lax.all_to_all(carried, "ctx", 0, 0, tiled=True)
    carried_in, carried_back = carried[:, :head_size], carried[:, head_size:]
    score_grad = (
        decay_table
        * jnp.einsum("htd,hsd->hts", grad_one, value_one, preferred_element_type=jnp.float32)
    ).astype(jnp.bfloat16)
    score_keys = (
        decay_table
        * jnp.einsum("htd,hsd->hts", query_one, key_one, preferred_element_type=jnp.float32)
    ).astype(jnp.bfloat16)
    query_new = jnp.einsum(
        "hts,hsd->htd", score_grad, key_one, preferred_element_type=jnp.float32
    ) + enter_weight[:, :, None] * jnp.einsum(
        "hte,hde->htd", grad_one, carried_in, preferred_element_type=jnp.float32
    )
    key_new = jnp.einsum(
        "hts,htd->hsd", score_grad, query_one, preferred_element_type=jnp.float32
    ) + leave_weight[:, :, None] * jnp.einsum(
        "hse,hde->hsd", value_one, carried_back, preferred_element_type=jnp.float32
    )
    value_new = jnp.einsum(
        "hts,htd->hsd", score_keys, grad_one, preferred_element_type=jnp.float32
    ) + leave_weight[:, :, None] * jnp.einsum(
        "hsd,hde->hse", key_one, carried_back, preferred_element_type=jnp.float32
    )
    query_grad = row_major(query_new, tok_rows, feature_width).reshape(1, tok_rows, feature_width)
    key_grad = row_major(key_new, tok_rows, feature_width).reshape(1, tok_rows, feature_width)
    value_grad = row_major(value_new, tok_rows, feature_width)
    token_all = lax.all_to_all(token_one, "ctx", 1, 0, tiled=True)
    token_all = lax.all_gather(token_all, "dp")
    value_all = lax.all_to_all(value_grad, "dp", 1, 0, tiled=True)
    value_all = lax.all_gather(value_all, "ctx")
    sequences = token_all.shape[0]
    token_all = token_all.reshape(sequences, groups, tok_rows, -1).transpose(1, 0, 2, 3)
    token_all = token_all.reshape(groups * sequences * tok_rows, -1)
    value_all = value_all.reshape(groups * sequences * tok_rows, -1)
    weight_grad = lax.dot_general(
        token_all, value_all, (((0,), (0,)), ((), ())), preferred_element_type=jnp.float32
    )
    return (query_grad, key_grad, weight_grad)


F32, BF16 = jnp.float32, jnp.bfloat16


def dot(left, right, left_dim, right_dim):
    return lax.dot_general(
        left, right, (((left_dim,), (right_dim,)), ((), ())), preferred_element_type=F32
    )


def push(src, dst, send_sem, recv_sem, dp, ctx):
    return pltpu.make_async_remote_copy(
        src_ref=src,
        dst_ref=dst,
        send_sem=send_sem,
        recv_sem=recv_sem,
        device_id=(dp, ctx),
        device_id_type=pl.DeviceIdType.MESH,
    )


def fused(
    planes, blocks, q, k, v, g, x, gate, bounds, qg, kg, wg,
    cum, decay_bias, enter_bias, leave_bias, through, xt_own, xt,
    local, mate_local, chip_state, arrived, carried, mate_carried, qi, ki, vi, vsend, vall,
    t_s, t_r, xa_s, xa_r, xz_s, xz_r, m1_s, m1_r, cs_s, cs_r, m2_s, m2_r, vz_s, vz_r,
    vb_s, vb_r, vm_s, vm_r,
):
    tok, feature = q.shape
    heads = gate.shape[0]
    size = feature // heads
    chunk = heads // planes
    half = chunk // 2
    rows = xt.shape[1]
    chips = blocks // 2
    d, c = lax.axis_index("dp"), lax.axis_index("ctx")
    core, chip = lax.rem(c, 2), lax.div(c, 2)
    mate = c + 1 - 2 * core
    first = core == 0

    barrier = pltpu.get_barrier_semaphore()
    for step in range(1, blocks):
        pl.semaphore_signal(
            barrier, inc=1, device_id=(d, lax.rem(c + step, blocks)),
            device_id_type=pl.DeviceIdType.MESH,
        )
    for step in range(1, planes):
        pl.semaphore_signal(
            barrier, inc=1, device_id=(lax.rem(d + step, planes), c),
            device_id_type=pl.DeviceIdType.MESH,
        )

    for part in range(x.shape[1] // 128):
        xt_own[part * 128 : (part + 1) * 128, :] = x[:, part * 128 : (part + 1) * 128].T
    pl.semaphore_wait(barrier, blocks - 1 + planes - 1)

    def columns(block):
        return pl.ds(pl.multiple_of(block * tok, tok), tok)

    def token_push(step):
        to = lax.rem(c + step, blocks)
        return push(
            xt_own.at[pl.ds(pl.multiple_of(to * rows, rows), rows), :],
            xt.at[d, :, columns(c)], xa_s.at[step - 1], xa_r.at[step - 1], d, to,
        )

    for step in range(1, blocks):
        token_push(step).start()
    xt[d, :, columns(c)] = xt_own[pl.ds(pl.multiple_of(c * rows, rows), rows), :]

    begin = c * tok
    at_t = lax.broadcasted_iota(jnp.int32, (tok, tok), 0)
    at_s = lax.broadcasted_iota(jnp.int32, (tok, tok), 1)
    seg_t = jnp.zeros((tok, tok), jnp.int32)
    seg_s = jnp.zeros((tok, tok), jnp.int32)
    seg_in = jnp.zeros((tok, tok), jnp.int32)
    seg_last = jnp.zeros((tok, tok), jnp.int32)
    for index in range(bounds.shape[1]):
        edge = jnp.full((tok, tok), bounds[0, index] - begin, jnp.int32)
        seg_t += (edge <= at_t).astype(jnp.int32)
        seg_s += (edge <= at_s).astype(jnp.int32)
        seg_in += (edge <= -1).astype(jnp.int32)
        seg_last += (edge <= tok - 1).astype(jnp.int32)
    decay_bias[...] = jnp.where((at_t >= at_s) & (seg_t == seg_s), 0.0, -1e30)
    enter_bias[...] = jnp.where(seg_t == seg_in, 0.0, -1e30)
    leave_bias[...] = jnp.where(seg_t == seg_last, 0.0, -1e30)
    cum[...] = lax.dot_general(
        gate[...], (at_t <= at_s).astype(F32), (((1,), (0,)), ((), ())),
        precision=lax.Precision.HIGHEST, preferred_element_type=F32,
    )
    total = jnp.broadcast_to(cum[:, tok - 1 : tok], (heads, size))
    through[c] = jnp.exp(total + enter_bias[tok - 1 : tok, :]).astype(BF16).astype(F32)

    def through_push(step):
        return push(
            through.at[c], through.at[c], t_s.at[step - 1], t_r.at[step - 1],
            d, lax.rem(c + step, blocks),
        )

    for step in range(1, blocks):
        through_push(step).start()

    def head_columns(head):
        return pl.ds(pl.multiple_of(head * size, size), size)

    def weights(head):
        at_row = jnp.broadcast_to(cum[pl.ds(head, 1), :], (size, tok))
        at_col = at_row.T
        enter = jnp.exp(at_col + enter_bias[...])
        leave = jnp.exp(at_col[tok - 1 : tok, :] - at_col + leave_bias[...])
        return at_row, at_col, enter, leave

    def chunk_head(i, j):
        return lax.rem(d + i, planes) * chunk + j

    def mate_push(i):
        return push(local.at[i, 1 - core], mate_local.at[i], m1_s.at[i], m1_r.at[i], d, mate)

    def halves(body):
        lax.fori_loop(0, 2, lambda part, carry: (body(part), carry)[1], 0)

    def local_chunk(i):
        def body(part):
            for j in range(half):
                head = chunk_head(i, part * half + j)
                cols = head_columns(head)
                _, _, enter, leave = weights(head)
                weighted_keys = (leave * k[:, cols].astype(F32)).astype(BF16)
                weighted_queries = (enter * q[:, cols].astype(F32)).astype(BF16)
                local[i, part, 0, j] = dot(weighted_keys, v[:, cols], 0, 0).astype(BF16)
                local[i, part, 1, j] = dot(weighted_queries, g[:, cols], 0, 0).astype(BF16)

        halves(body)
        mate_push(i).start()

    def through_wait():
        for step in range(1, blocks):
            frm = lax.rem(c - step + blocks, blocks)
            push(
                through.at[frm], through.at[frm], t_s.at[step - 1], t_r.at[step - 1], d, frm
            ).wait_recv()

    def state_push(i, step):
        ahead = chip + step
        return push(
            chip_state.at[i, lax.div(ahead, chips)], arrived.at[i, step - 1],
            cs_s.at[i, step - 1], cs_r.at[i, step - 1], d, 2 * lax.rem(ahead, chips) + core,
        )

    def chip_chunk(i):
        mate_push(i).wait_recv()
        for j in range(half):
            head = chunk_head(i, core * half + j)
            mine = through[c, pl.ds(head, 1), :]
            other = through[mate, pl.ds(head, 1), :]
            chip_state[i, 0, j] = (
                jnp.where(first, other, 1.0) * local[i, core, 0, j].astype(F32)
                + jnp.where(first, 1.0, mine) * mate_local[i, 0, j].astype(F32)
            ).astype(BF16)
            chip_state[i, 1, j] = (
                jnp.where(first, 1.0, other) * local[i, core, 1, j].astype(F32)
                + jnp.where(first, mine, 1.0) * mate_local[i, 1, j].astype(F32)
            ).astype(BF16)
        for step in range(1, chips):
            state_push(i, step).start()

    def token_wait():
        for step in range(1, blocks):
            token_push(step).wait_send()
            frm = lax.rem(c - step + blocks, blocks)
            push(
                xt.at[d, :, columns(frm)], xt.at[d, :, columns(frm)],
                xa_s.at[step - 1], xa_r.at[step - 1], d, frm,
            ).wait_recv()

    def chain(step, act):
        @pl.when((d >= step - 1) & (d + 1 < planes))
        def _():
            piece = xt.at[d - (step - 1)]
            act(push(piece, piece, xz_s.at[0, step - 1], xz_r.at[0, step - 1], d + 1, c))

        @pl.when((d + step - 1 < planes) & (d >= 1))
        def _():
            piece = xt.at[d + step - 1]
            act(push(piece, piece, xz_s.at[1, step - 1], xz_r.at[1, step - 1], d - 1, c))

    def chain_wait(step):
        @pl.when(d >= step)
        def _():
            piece = xt.at[d - step]
            push(piece, piece, xz_s.at[0, step - 1], xz_r.at[0, step - 1], d - 1, c).wait_recv()

        @pl.when(d + step < planes)
        def _():
            piece = xt.at[d + step]
            push(piece, piece, xz_s.at[1, step - 1], xz_r.at[1, step - 1], d + 1, c).wait_recv()

    def inner_chunk(i):
        def body(part):
            for j in range(half):
                head = chunk_head(i, part * half + j)
                cols = head_columns(head)
                at_row = jnp.broadcast_to(cum[pl.ds(head, 1), :], (size, tok))
                decay = jnp.exp(at_row.T - at_row + decay_bias[...])
                qh, kh, vh, gh = q[:, cols], k[:, cols], v[:, cols], g[:, cols]
                score_grad = (decay * dot(gh, vh, 1, 1)).astype(BF16)
                score_keys = (decay * dot(qh, kh, 1, 1)).astype(BF16)
                qi[:, cols] = dot(score_grad, kh, 1, 0)
                ki[:, cols] = dot(score_grad, qh, 0, 0)
                vi[:, cols] = dot(score_keys, gh, 0, 0)

        halves(body)

    def carried_push(i):
        return push(mate_carried.at[i], carried.at[i, core], m2_s.at[i], m2_r.at[i], d, mate)

    def carry_chunk(i):
        for step in range(1, chips):
            state_push(i, step).wait_recv()
        for j in range(half):
            head = chunk_head(i, core * half + j)
            mine = through[c, pl.ds(head, 1), :]
            other = through[mate, pl.ds(head, 1), :]
            sums = []
            for back in (False, True):
                state = jnp.zeros((size, size), F32)
                weight = jnp.ones((1, size), F32)
                for far in range(1, chips):
                    if back:
                        valid = chip + far < chips
                        source, slot = lax.rem(chip + far, chips), chips - far - 1
                    else:
                        valid = chip >= far
                        source, slot = lax.rem(chip - far + chips, chips), far - 1
                    state += jnp.where(valid, weight, 0.0) * arrived[i, slot, j].astype(F32)
                    weight = weight * (
                        through[2 * source, pl.ds(head, 1), :]
                        * through[2 * source + 1, pl.ds(head, 1), :]
                    )
                sums.append(state)
            came, back = sums
            late = jnp.where(first, 0.0, 1.0)
            early = 1.0 - late
            carried[i, core, 0, j] = (
                jnp.where(first, 1.0, other) * came + late * mate_local[i, 0, j].astype(F32)
            ).astype(BF16)
            carried[i, core, 1, j] = (
                jnp.where(first, other, 1.0) * back + early * mate_local[i, 1, j].astype(F32)
            ).astype(BF16)
            mate_carried[i, 0, j] = (
                jnp.where(first, mine, 1.0) * came + early * local[i, core, 0, j].astype(F32)
            ).astype(BF16)
            mate_carried[i, 1, j] = (
                jnp.where(first, 1.0, mine) * back + late * local[i, core, 1, j].astype(F32)
            ).astype(BF16)
        carried_push(i).start()

    def value_push(i):
        return push(
            vsend.at[i], vall.at[d, c], vz_s.at[i], vz_r.at[i], lax.rem(d + i, planes), c
        )

    def finish(i):
        push(
            carried.at[i, 1 - core], carried.at[i, 1 - core], m2_s.at[i], m2_r.at[i], d, mate
        ).wait_recv()
        def body(part):
            for j in range(half):
                head = chunk_head(i, part * half + j)
                cols = head_columns(head)
                _, _, enter, leave = weights(head)
                came, back = carried[i, part, 0, j], carried[i, part, 1, j]
                vsend[i, :, head_columns(part * half + j)] = (
                    vi[:, cols] + leave * dot(k[:, cols], back, 1, 0)
                ).astype(BF16)
                qg[:, cols] = (qi[:, cols] + enter * dot(g[:, cols], came, 1, 1)).astype(BF16)
                kg[:, cols] = (ki[:, cols] + leave * dot(v[:, cols], back, 1, 1)).astype(BF16)

        halves(body)
        if i == 0:
            vall[d, c] = vsend[0]
        else:
            value_push(i).start()

    def source_plane(i):
        return lax.rem(d - i + planes, planes)

    def spread(i, act):
        piece = vall.at[source_plane(i), c]
        for step in range(1, chips):
            to = 2 * lax.rem(chip + step, chips) + core
            act(push(piece, piece, vb_s.at[i, step - 1], vb_r.at[i, step - 1], d, to))
        act(push(piece, piece, vm_s.at[i, 0], vm_r.at[i, 0], d, mate))

    def receive(i):
        if i:
            piece = vall.at[source_plane(i), c]
            push(piece, piece, vz_s.at[i], vz_r.at[i], source_plane(i), c).wait_recv()
        spread(i, lambda copy: copy.start())

    def forward(i, act, wait):
        for step in range(1, chips):
            frm = 2 * lax.rem(chip - step + chips, chips) + core
            piece = vall.at[source_plane(i), frm]
            if wait:
                push(
                    piece, piece, vb_s.at[i, step - 1], vb_r.at[i, step - 1], d, frm
                ).wait_recv()
            act(push(piece, piece, vm_s.at[i, step], vm_r.at[i, step], d, mate))

    def multiply(i):
        plane = source_plane(i)
        for step in range(chips):
            frm = 2 * lax.rem(chip - step + chips, chips) + 1 - core
            piece = vall.at[plane, frm]
            push(piece, piece, vm_s.at[i, step], vm_r.at[i, step], d, mate).wait_recv()
        width = 256

        def tile(index, carry):
            cols = pl.ds(pl.multiple_of(index * width, width), width)
            right = vall[plane, :, :, cols].reshape(blocks * tok, width)
            product = dot(xt[plane], right, 1, 0)
            wg[:, cols] = product if i == 0 else wg[:, cols] + product
            return carry

        lax.fori_loop(0, wg.shape[1] // width, tile, 0)

    start = lambda copy: copy.start()
    last = planes - 1

    local_chunk(0)
    for i in range(1, planes + 1):
        if i < planes:
            local_chunk(i)
        if i == 1:
            through_wait()
        chip_chunk(i - 1)
        if i == min(2, planes):
            token_wait()
            chain(1, start)
    inner_chunk(0)
    carry_chunk(0)
    done = 1
    for i in range(planes):
        if i < last:
            inner_chunk(i + 1)
        finish(i)
        if i == 0:
            receive(0)
        elif i > 1:
            receive(i - 1)
            forward(i - 2, start, True)
        if done < last and i in (0, 2):
            chain_wait(done)
            done += 1
            chain(done, start)
        if i < last:
            carry_chunk(i + 1)
    while done < last:
        chain_wait(done)
        done += 1
        chain(done, start)
    receive(last)
    forward(last - 1, start, True)
    multiply(0)
    forward(last, start, True)
    chain_wait(done)
    for i in range(1, planes):
        multiply(i)

    for step in range(1, blocks):
        through_push(step).wait_send()
    for step in range(1, planes):
        chain(step, lambda copy: copy.wait_send())
    for i in range(planes):
        mate_push(i).wait_send()
        carried_push(i).wait_send()
        for step in range(1, chips):
            state_push(i, step).wait_send()
        if i:
            value_push(i).wait_send()
        spread(i, lambda copy: copy.wait_send())
        forward(i, lambda copy: copy.wait_send(), False)


def per_device_fused(planes, blocks, inputs, queries, keys, values, out_grad, log_gate, boundaries):
    tok, feature = queries.shape[1:]
    heads = log_gate.shape[1]
    size = feature // heads
    chunk = heads // planes
    half = chunk // 2
    chips = blocks // 2
    width = feature // planes
    rows = inputs.shape[2] // blocks
    vmem = pl.BlockSpec(memory_space=pltpu.VMEM)
    sem = pltpu.SemaphoreType.DMA
    scratch = [
        pltpu.VMEM((heads, tok), F32),
        pltpu.VMEM((tok, tok), F32),
        pltpu.VMEM((tok, tok), F32),
        pltpu.VMEM((tok, tok), F32),
        pltpu.VMEM((blocks, heads, size), F32),
        pltpu.VMEM((inputs.shape[2], tok), BF16),
        pltpu.VMEM((planes, rows, blocks * tok), BF16),
        pltpu.VMEM((planes, 2, 2, half, size, size), BF16),
        pltpu.VMEM((planes, 2, half, size, size), BF16),
        pltpu.VMEM((planes, 2, half, size, size), BF16),
        pltpu.VMEM((planes, chips - 1, half, size, size), BF16),
        pltpu.VMEM((planes, 2, 2, half, size, size), BF16),
        pltpu.VMEM((planes, 2, half, size, size), BF16),
        pltpu.VMEM((tok, feature), F32),
        pltpu.VMEM((tok, feature), F32),
        pltpu.VMEM((tok, feature), F32),
        pltpu.VMEM((planes, tok, width), BF16),
        pltpu.VMEM((planes, blocks, tok, width), BF16),
        sem((blocks - 1,)), sem((blocks - 1,)),
        sem((blocks - 1,)), sem((blocks - 1,)),
        sem((2, planes - 1)), sem((2, planes - 1)),
        sem((planes,)), sem((planes,)),
        sem((planes, chips - 1)), sem((planes, chips - 1)),
        sem((planes,)), sem((planes,)),
        sem((planes,)), sem((planes,)),
        sem((planes, chips - 1)), sem((planes, chips - 1)),
        sem((planes, chips)), sem((planes, chips)),
    ]
    query_grad, key_grad, weight_grad = pl.pallas_call(
        functools.partial(fused, planes, blocks),
        out_shape=(
            jax.ShapeDtypeStruct((tok, feature), BF16),
            jax.ShapeDtypeStruct((tok, feature), BF16),
            jax.ShapeDtypeStruct((rows, width), F32),
        ),
        in_specs=[vmem] * 6 + [pl.BlockSpec(memory_space=pltpu.SMEM)],
        out_specs=(vmem, vmem, vmem),
        scratch_shapes=scratch,
        compiler_params=pltpu.CompilerParams(
            collective_id=0, has_side_effects=True, vmem_limit_bytes=VMEM_LIMIT
        ),
    )(queries[0], keys[0], values[0], out_grad[0], inputs[0], log_gate[0], boundaries)
    return query_grad[None], key_grad[None], weight_grad


VMEM_LIMIT = 60 * 2**20


def per_device(mesh, inputs, queries, keys, values, out_grad, log_gate, boundaries):
    planes, blocks = mesh.shape["dp"], mesh.shape["ctx"]
    arrays = (inputs, queries, keys, values, out_grad, log_gate, boundaries)
    tok, feature = queries.shape[1:]
    gathered = 2 * planes * blocks * tok * (feature // planes + inputs.shape[2] // blocks)
    if gathered + 32 * tok * feature * 2 > VMEM_LIMIT:
        return per_device_plain(*arrays)
    return per_device_fused(planes, blocks, *arrays)


def solution(mesh):
    in_specs = (
        P("dp", "ctx", None),
        P("dp", "ctx", None),
        P("dp", "ctx", None),
        P("dp", "ctx", None),
        P("dp", "ctx", None),
        P("dp", None, "ctx"),
        P("dp", None),
    )
    out_specs = (P("dp", "ctx", None), P("dp", "ctx", None), P("ctx", "dp"))
    return jax.shard_map(
        functools.partial(per_device, mesh), mesh=mesh, in_specs=in_specs, out_specs=out_specs, check_vma=False
    )
```

```python
import functools

import jax
import jax.numpy as jnp
from jax import lax
from jax.experimental import pallas as pl
from jax.experimental.pallas import tpu as pltpu
from jax.sharding import PartitionSpec as P


def head_major(array, tok_rows, head_count, head_size):
    return array[0].reshape(tok_rows, head_count, head_size).transpose(1, 0, 2)


def row_major(array, tok_rows, feature_width):
    return array.astype(jnp.bfloat16).transpose(1, 0, 2).reshape(tok_rows, feature_width)


def per_device_plain(inputs, queries, keys, values, out_grad, log_gate, boundaries):
    tok_rows = queries.shape[1]
    feature_width = queries.shape[2]
    head_count = log_gate.shape[1]
    head_size = feature_width // head_count
    query_one = head_major(queries, tok_rows, head_count, head_size)
    key_one = head_major(keys, tok_rows, head_count, head_size)
    value_one = head_major(values, tok_rows, head_count, head_size)
    grad_one = head_major(out_grad, tok_rows, head_count, head_size)
    token_one = inputs[0]
    bounds = boundaries[0]
    begin_at = lax.axis_index("ctx") * tok_rows
    positions = begin_at + jnp.arange(tok_rows, dtype=jnp.int32)
    segment_ids = jnp.sum((bounds[None, :] <= positions[:, None]).astype(jnp.int32), axis=1)
    segment_in = jnp.sum((bounds <= begin_at - 1).astype(jnp.int32))
    cumulative = jnp.cumsum(log_gate[0], axis=1)
    enter_weight = jnp.where((segment_ids == segment_in)[None, :], jnp.exp(cumulative), 0.0)
    leave_weight = jnp.where(
        (segment_ids == segment_ids[-1])[None, :], jnp.exp(cumulative[:, -1:] - cumulative), 0.0
    )
    causal = (positions[:, None] >= positions[None, :]) & (
        segment_ids[:, None] == segment_ids[None, :]
    )
    decay_table = jnp.exp(
        jnp.where(causal[None], cumulative[:, :, None] - cumulative[:, None, :], -1e30)
    )
    through = enter_weight[:, -1].astype(jnp.bfloat16)
    weighted_keys = (leave_weight[:, :, None] * key_one).astype(jnp.bfloat16)
    local_state = jnp.einsum(
        "hsd,hse->hde", weighted_keys, value_one, preferred_element_type=jnp.float32
    )
    weighted_queries = (enter_weight[:, :, None] * query_one).astype(jnp.bfloat16)
    back_state = jnp.einsum(
        "htd,hte->hde", weighted_queries, grad_one, preferred_element_type=jnp.float32
    )
    groups = lax.axis_size("ctx")
    extra = jnp.broadcast_to(through[:, None, None], (head_count, 16, head_size))
    packed = jnp.concatenate(
        [local_state.astype(jnp.bfloat16), back_state.astype(jnp.bfloat16), extra], axis=1
    )
    packed = lax.all_to_all(packed, "ctx", 0, 0, tiled=True)
    packed = packed.reshape(groups, head_count // groups, 2 * head_size + 16, head_size)
    ahead = packed[:, :, :head_size].astype(jnp.float32)
    behind = packed[:, :, head_size : 2 * head_size].astype(jnp.float32)
    factor = packed[:, :, 2 * head_size, :1, None].astype(jnp.float32)
    state_in = [jnp.zeros_like(ahead[0])]
    state_back = [jnp.zeros_like(ahead[0])]
    for block in range(groups - 1):
        state_in.append(factor[block] * state_in[-1] + ahead[block])
        late = groups - 1 - block
        state_back.append(factor[late] * state_back[-1] + behind[late])
    carried = jnp.concatenate([jnp.stack(state_in), jnp.stack(state_back[::-1])], axis=2)
    carried = carried.astype(jnp.bfloat16).reshape(head_count, 2 * head_size, head_size)
    carried = lax.all_to_all(carried, "ctx", 0, 0, tiled=True)
    carried_in, carried_back = carried[:, :head_size], carried[:, head_size:]
    score_grad = (
        decay_table
        * jnp.einsum("htd,hsd->hts", grad_one, value_one, preferred_element_type=jnp.float32)
    ).astype(jnp.bfloat16)
    score_keys = (
        decay_table
        * jnp.einsum("htd,hsd->hts", query_one, key_one, preferred_element_type=jnp.float32)
    ).astype(jnp.bfloat16)
    query_new = jnp.einsum(
        "hts,hsd->htd", score_grad, key_one, preferred_element_type=jnp.float32
    ) + enter_weight[:, :, None] * jnp.einsum(
        "hte,hde->htd", grad_one, carried_in, preferred_element_type=jnp.float32
    )
    key_new = jnp.einsum(
        "hts,htd->hsd", score_grad, query_one, preferred_element_type=jnp.float32
    ) + leave_weight[:, :, None] * jnp.einsum(
        "hse,hde->hsd", value_one, carried_back, preferred_element_type=jnp.float32
    )
    value_new = jnp.einsum(
        "hts,htd->hsd", score_keys, grad_one, preferred_element_type=jnp.float32
    ) + leave_weight[:, :, None] * jnp.einsum(
        "hsd,hde->hse", key_one, carried_back, preferred_element_type=jnp.float32
    )
    query_grad = row_major(query_new, tok_rows, feature_width).reshape(1, tok_rows, feature_width)
    key_grad = row_major(key_new, tok_rows, feature_width).reshape(1, tok_rows, feature_width)
    value_grad = row_major(value_new, tok_rows, feature_width)
    token_all = lax.all_to_all(token_one, "ctx", 1, 0, tiled=True)
    token_all = lax.all_gather(token_all, "dp")
    value_all = lax.all_to_all(value_grad, "dp", 1, 0, tiled=True)
    value_all = lax.all_gather(value_all, "ctx")
    sequences = token_all.shape[0]
    token_all = token_all.reshape(sequences, groups, tok_rows, -1).transpose(1, 0, 2, 3)
    token_all = token_all.reshape(groups * sequences * tok_rows, -1)
    value_all = value_all.reshape(groups * sequences * tok_rows, -1)
    weight_grad = lax.dot_general(
        token_all, value_all, (((0,), (0,)), ((), ())), preferred_element_type=jnp.float32
    )
    return (query_grad, key_grad, weight_grad)


F32, BF16 = jnp.float32, jnp.bfloat16


def dot(left, right, left_dim, right_dim):
    return lax.dot_general(
        left, right, (((left_dim,), (right_dim,)), ((), ())), preferred_element_type=F32
    )


def push(src, dst, send_sem, recv_sem, dp, ctx):
    return pltpu.make_async_remote_copy(
        src_ref=src,
        dst_ref=dst,
        send_sem=send_sem,
        recv_sem=recv_sem,
        device_id=(dp, ctx),
        device_id_type=pl.DeviceIdType.MESH,
    )


def fused(
    planes, blocks, q, k, v, g, x, gate, bounds, qg, kg, wg,
    cum, decay_bias, enter_bias, leave_bias, through, xt_own, xt,
    local, mate_local, chip_state, arrived, carried, mate_carried, qi, ki, vi, vsend, vall,
    t_s, t_r, xa_s, xa_r, xz_s, xz_r, m1_s, m1_r, cs_s, cs_r, m2_s, m2_r, vz_s, vz_r,
    vb_s, vb_r, vm_s, vm_r,
):
    tok, feature = q.shape
    heads = gate.shape[0]
    size = feature // heads
    chunk = heads // planes
    half = chunk // 2
    rows = xt.shape[1]
    chips = blocks // 2
    d, c = lax.axis_index("dp"), lax.axis_index("ctx")
    core, chip = lax.rem(c, 2), lax.div(c, 2)
    mate = c + 1 - 2 * core
    first = core == 0

    barrier = pltpu.get_barrier_semaphore()
    for step in range(1, blocks):
        pl.semaphore_signal(
            barrier, inc=1, device_id=(d, lax.rem(c + step, blocks)),
            device_id_type=pl.DeviceIdType.MESH,
        )
    for step in range(1, planes):
        pl.semaphore_signal(
            barrier, inc=1, device_id=(lax.rem(d + step, planes), c),
            device_id_type=pl.DeviceIdType.MESH,
        )

    for part in range(x.shape[1] // 128):
        xt_own[part * 128 : (part + 1) * 128, :] = x[:, part * 128 : (part + 1) * 128].T
    pl.semaphore_wait(barrier, blocks - 1 + planes - 1)

    def columns(block):
        return pl.ds(pl.multiple_of(block * tok, tok), tok)

    def token_push(step):
        to = lax.rem(c + step, blocks)
        return push(
            xt_own.at[pl.ds(pl.multiple_of(to * rows, rows), rows), :],
            xt.at[d, :, columns(c)], xa_s.at[step - 1], xa_r.at[step - 1], d, to,
        )

    for step in range(1, blocks):
        token_push(step).start()
    xt[d, :, columns(c)] = xt_own[pl.ds(pl.multiple_of(c * rows, rows), rows), :]

    begin = c * tok
    at_t = lax.broadcasted_iota(jnp.int32, (tok, tok), 0)
    at_s = lax.broadcasted_iota(jnp.int32, (tok, tok), 1)
    seg_t = jnp.zeros((tok, tok), jnp.int32)
    seg_s = jnp.zeros((tok, tok), jnp.int32)
    seg_in = jnp.zeros((tok, tok), jnp.int32)
    seg_last = jnp.zeros((tok, tok), jnp.int32)
    for index in range(bounds.shape[1]):
        edge = jnp.full((tok, tok), bounds[0, index] - begin, jnp.int32)
        seg_t += (edge <= at_t).astype(jnp.int32)
        seg_s += (edge <= at_s).astype(jnp.int32)
        seg_in += (edge <= -1).astype(jnp.int32)
        seg_last += (edge <= tok - 1).astype(jnp.int32)
    decay_bias[...] = jnp.where((at_t >= at_s) & (seg_t == seg_s), 0.0, -1e30)
    enter_bias[...] = jnp.where(seg_t == seg_in, 0.0, -1e30)
    leave_bias[...] = jnp.where(seg_t == seg_last, 0.0, -1e30)
    cum[...] = lax.dot_general(
        gate[...], (at_t <= at_s).astype(F32), (((1,), (0,)), ((), ())),
        precision=lax.Precision.HIGHEST, preferred_element_type=F32,
    )
    total = jnp.broadcast_to(cum[:, tok - 1 : tok], (heads, size))
    through[c] = jnp.exp(total + enter_bias[tok - 1 : tok, :]).astype(BF16).astype(F32)

    def through_push(step):
        return push(
            through.at[c], through.at[c], t_s.at[step - 1], t_r.at[step - 1],
            d, lax.rem(c + step, blocks),
        )

    for step in range(1, blocks):
        through_push(step).start()

    def head_columns(head):
        return pl.ds(pl.multiple_of(head * size, size), size)

    def weights(head):
        at_row = jnp.broadcast_to(cum[pl.ds(head, 1), :], (size, tok))
        at_col = at_row.T
        enter = jnp.exp(at_col + enter_bias[...])
        leave = jnp.exp(at_col[tok - 1 : tok, :] - at_col + leave_bias[...])
        return at_row, at_col, enter, leave

    def chunk_head(i, j):
        return lax.rem(d + i, planes) * chunk + j

    def mate_push(i):
        return push(local.at[i, 1 - core], mate_local.at[i], m1_s.at[i], m1_r.at[i], d, mate)

    def halves(body):
        lax.fori_loop(0, 2, lambda part, carry: (body(part), carry)[1], 0)

    def local_chunk(i):
        def body(part):
            for j in range(half):
                head = chunk_head(i, part * half + j)
                cols = head_columns(head)
                _, _, enter, leave = weights(head)
                weighted_keys = (leave * k[:, cols].astype(F32)).astype(BF16)
                weighted_queries = (enter * q[:, cols].astype(F32)).astype(BF16)
                local[i, part, 0, j] = dot(weighted_keys, v[:, cols], 0, 0).astype(BF16)
                local[i, part, 1, j] = dot(weighted_queries, g[:, cols], 0, 0).astype(BF16)

        halves(body)
        mate_push(i).start()

    def through_wait():
        for step in range(1, blocks):
            frm = lax.rem(c - step + blocks, blocks)
            push(
                through.at[frm], through.at[frm], t_s.at[step - 1], t_r.at[step - 1], d, frm
            ).wait_recv()

    def state_push(i, step):
        ahead = chip + step
        return push(
            chip_state.at[i, lax.div(ahead, chips)], arrived.at[i, step - 1],
            cs_s.at[i, step - 1], cs_r.at[i, step - 1], d, 2 * lax.rem(ahead, chips) + core,
        )

    def chip_chunk(i):
        mate_push(i).wait_recv()
        for j in range(half):
            head = chunk_head(i, core * half + j)
            mine = through[c, pl.ds(head, 1), :]
            other = through[mate, pl.ds(head, 1), :]
            chip_state[i, 0, j] = (
                jnp.where(first, other, 1.0) * local[i, core, 0, j].astype(F32)
                + jnp.where(first, 1.0, mine) * mate_local[i, 0, j].astype(F32)
            ).astype(BF16)
            chip_state[i, 1, j] = (
                jnp.where(first, 1.0, other) * local[i, core, 1, j].astype(F32)
                + jnp.where(first, mine, 1.0) * mate_local[i, 1, j].astype(F32)
            ).astype(BF16)
        for step in range(1, chips):
            state_push(i, step).start()

    def token_wait():
        for step in range(1, blocks):
            token_push(step).wait_send()
            frm = lax.rem(c - step + blocks, blocks)
            push(
                xt.at[d, :, columns(frm)], xt.at[d, :, columns(frm)],
                xa_s.at[step - 1], xa_r.at[step - 1], d, frm,
            ).wait_recv()

    def chain(step, act):
        @pl.when((d >= step - 1) & (d + 1 < planes))
        def _():
            piece = xt.at[d - (step - 1)]
            act(push(piece, piece, xz_s.at[0, step - 1], xz_r.at[0, step - 1], d + 1, c))

        @pl.when((d + step - 1 < planes) & (d >= 1))
        def _():
            piece = xt.at[d + step - 1]
            act(push(piece, piece, xz_s.at[1, step - 1], xz_r.at[1, step - 1], d - 1, c))

    def chain_wait(step):
        @pl.when(d >= step)
        def _():
            piece = xt.at[d - step]
            push(piece, piece, xz_s.at[0, step - 1], xz_r.at[0, step - 1], d - 1, c).wait_recv()

        @pl.when(d + step < planes)
        def _():
            piece = xt.at[d + step]
            push(piece, piece, xz_s.at[1, step - 1], xz_r.at[1, step - 1], d + 1, c).wait_recv()

    def inner_chunk(i):
        def body(part):
            for j in range(half):
                head = chunk_head(i, part * half + j)
                cols = head_columns(head)
                at_row = jnp.broadcast_to(cum[pl.ds(head, 1), :], (size, tok))
                decay = jnp.exp(at_row.T - at_row + decay_bias[...])
                qh, kh, vh, gh = q[:, cols], k[:, cols], v[:, cols], g[:, cols]
                score_grad = (decay * dot(gh, vh, 1, 1)).astype(BF16)
                score_keys = (decay * dot(qh, kh, 1, 1)).astype(BF16)
                qi[:, cols] = dot(score_grad, kh, 1, 0)
                ki[:, cols] = dot(score_grad, qh, 0, 0)
                vi[:, cols] = dot(score_keys, gh, 0, 0)

        halves(body)

    def carried_push(i):
        return push(mate_carried.at[i], carried.at[i, core], m2_s.at[i], m2_r.at[i], d, mate)

    def carry_chunk(i):
        for step in range(1, chips):
            state_push(i, step).wait_recv()
        for j in range(half):
            head = chunk_head(i, core * half + j)
            mine = through[c, pl.ds(head, 1), :]
            other = through[mate, pl.ds(head, 1), :]
            sums = []
            for back in (False, True):
                state = jnp.zeros((size, size), F32)
                weight = jnp.ones((1, size), F32)
                for far in range(1, chips):
                    if back:
                        valid = chip + far < chips
                        source, slot = lax.rem(chip + far, chips), chips - far - 1
                    else:
                        valid = chip >= far
                        source, slot = lax.rem(chip - far + chips, chips), far - 1
                    state += jnp.where(valid, weight, 0.0) * arrived[i, slot, j].astype(F32)
                    weight = weight * (
                        through[2 * source, pl.ds(head, 1), :]
                        * through[2 * source + 1, pl.ds(head, 1), :]
                    )
                sums.append(state)
            came, back = sums
            late = jnp.where(first, 0.0, 1.0)
            early = 1.0 - late
            carried[i, core, 0, j] = (
                jnp.where(first, 1.0, other) * came + late * mate_local[i, 0, j].astype(F32)
            ).astype(BF16)
            carried[i, core, 1, j] = (
                jnp.where(first, other, 1.0) * back + early * mate_local[i, 1, j].astype(F32)
            ).astype(BF16)
            mate_carried[i, 0, j] = (
                jnp.where(first, mine, 1.0) * came + early * local[i, core, 0, j].astype(F32)
            ).astype(BF16)
            mate_carried[i, 1, j] = (
                jnp.where(first, 1.0, mine) * back + late * local[i, core, 1, j].astype(F32)
            ).astype(BF16)
        carried_push(i).start()

    def value_push(i):
        return push(
            vsend.at[i], vall.at[d, c], vz_s.at[i], vz_r.at[i], lax.rem(d + i, planes), c
        )

    def finish(i):
        push(
            carried.at[i, 1 - core], carried.at[i, 1 - core], m2_s.at[i], m2_r.at[i], d, mate
        ).wait_recv()
        def body(part):
            for j in range(half):
                head = chunk_head(i, part * half + j)
                cols = head_columns(head)
                _, _, enter, leave = weights(head)
                came, back = carried[i, part, 0, j], carried[i, part, 1, j]
                vsend[i, :, head_columns(part * half + j)] = (
                    vi[:, cols] + leave * dot(k[:, cols], back, 1, 0)
                ).astype(BF16)
                qg[:, cols] = (qi[:, cols] + enter * dot(g[:, cols], came, 1, 1)).astype(BF16)
                kg[:, cols] = (ki[:, cols] + leave * dot(v[:, cols], back, 1, 1)).astype(BF16)

        halves(body)
        if i == 0:
            vall[d, c] = vsend[0]
        else:
            value_push(i).start()

    def source_plane(i):
        return lax.rem(d - i + planes, planes)

    across = chip + 1 - 2 * lax.rem(chip, 2)
    along = lax.rem(chip + 2, chips)
    corner = chips - 1 - chip

    def spread(i, act):
        piece = vall.at[source_plane(i), c]
        for slot, to in enumerate((across, along)):
            act(push(piece, piece, vb_s.at[i, slot], vb_r.at[i, slot], d, 2 * to + core))
        act(push(piece, piece, vm_s.at[i, 0], vm_r.at[i, 0], d, mate))

    def receive(i):
        if i:
            piece = vall.at[source_plane(i), c]
            push(piece, piece, vz_s.at[i], vz_r.at[i], source_plane(i), c).wait_recv()
        spread(i, lambda copy: copy.start())

    def forward(i, act, wait):
        for slot, (frm, to) in enumerate(((across, along), (along, across))):
            piece = vall.at[source_plane(i), 2 * frm + core]
            if wait:
                push(
                    piece, piece, vb_s.at[i, slot], vb_r.at[i, slot], d, 2 * frm + core
                ).wait_recv()
            part = vall.at[source_plane(i), 2 * frm + core, pl.ds(slot * (tok // 2), tok // 2), :]
            act(push(part, part, vb_s.at[i, 2 + slot], vb_r.at[i, 2 + slot], d, 2 * to + core))
            act(push(piece, piece, vm_s.at[i, 1 + slot], vm_r.at[i, 1 + slot], d, mate))

    def forward_corner(i, act, wait):
        frm = 2 * corner + core
        if wait:
            for slot, via in enumerate((along, across)):
                part = vall.at[source_plane(i), frm, pl.ds(slot * (tok // 2), tok // 2), :]
                push(
                    part, part, vb_s.at[i, 2 + slot], vb_r.at[i, 2 + slot], d, 2 * via + core
                ).wait_recv()
        piece = vall.at[source_plane(i), frm]
        act(push(piece, piece, vm_s.at[i, 3], vm_r.at[i, 3], d, mate))

    def multiply(i):
        plane = source_plane(i)
        for slot, frm in enumerate((chip, across, along, corner)):
            piece = vall.at[plane, 2 * frm + 1 - core]
            push(piece, piece, vm_s.at[i, slot], vm_r.at[i, slot], d, mate).wait_recv()
        width = 256

        def tile(index, carry):
            cols = pl.ds(pl.multiple_of(index * width, width), width)
            right = vall[plane, :, :, cols].reshape(blocks * tok, width)
            product = dot(xt[plane], right, 1, 0)
            wg[:, cols] = product if i == 0 else wg[:, cols] + product
            return carry

        lax.fori_loop(0, wg.shape[1] // width, tile, 0)

    start = lambda copy: copy.start()
    last = planes - 1

    local_chunk(0)
    for i in range(1, planes + 1):
        if i < planes:
            local_chunk(i)
        if i == 1:
            through_wait()
        chip_chunk(i - 1)
        if i == min(2, planes):
            token_wait()
            chain(1, start)
    inner_chunk(0)
    carry_chunk(0)
    for i in range(planes):
        if i < last:
            inner_chunk(i + 1)
        if i == 0:
            chain_wait(1)
            chain(2, start)
        finish(i)
        if i == 0:
            receive(0)
        elif i == 1:
            forward(0, start, True)
        else:
            if i == last:
                for step in range(2, last):
                    chain_wait(step)
                    chain(step + 1, start)
            receive(i - 1)
            if i == 2:
                forward_corner(0, start, True)
            else:
                forward(i - 2, start, True)
        if i < last:
            carry_chunk(i + 1)
    receive(last)
    forward(last - 1, start, True)
    for i in range(1, last):
        forward_corner(i, start, True)
    multiply(0)
    forward(last, start, True)
    forward_corner(last, start, True)
    chain_wait(last)
    for i in range(1, planes):
        multiply(i)

    for step in range(1, blocks):
        through_push(step).wait_send()
    for step in range(1, planes):
        chain(step, lambda copy: copy.wait_send())
    for i in range(planes):
        mate_push(i).wait_send()
        carried_push(i).wait_send()
        for step in range(1, chips):
            state_push(i, step).wait_send()
        if i:
            value_push(i).wait_send()
        spread(i, lambda copy: copy.wait_send())
        forward(i, lambda copy: copy.wait_send(), False)
        forward_corner(i, lambda copy: copy.wait_send(), False)


def per_device_fused(planes, blocks, inputs, queries, keys, values, out_grad, log_gate, boundaries):
    tok, feature = queries.shape[1:]
    heads = log_gate.shape[1]
    size = feature // heads
    chunk = heads // planes
    half = chunk // 2
    chips = blocks // 2
    width = feature // planes
    rows = inputs.shape[2] // blocks
    vmem = pl.BlockSpec(memory_space=pltpu.VMEM)
    sem = pltpu.SemaphoreType.DMA
    scratch = [
        pltpu.VMEM((heads, tok), F32),
        pltpu.VMEM((tok, tok), F32),
        pltpu.VMEM((tok, tok), F32),
        pltpu.VMEM((tok, tok), F32),
        pltpu.VMEM((blocks, heads, size), F32),
        pltpu.VMEM((inputs.shape[2], tok), BF16),
        pltpu.VMEM((planes, rows, blocks * tok), BF16),
        pltpu.VMEM((planes, 2, 2, half, size, size), BF16),
        pltpu.VMEM((planes, 2, half, size, size), BF16),
        pltpu.VMEM((planes, 2, half, size, size), BF16),
        pltpu.VMEM((planes, chips - 1, half, size, size), BF16),
        pltpu.VMEM((planes, 2, 2, half, size, size), BF16),
        pltpu.VMEM((planes, 2, half, size, size), BF16),
        pltpu.VMEM((tok, feature), F32),
        pltpu.VMEM((tok, feature), F32),
        pltpu.VMEM((tok, feature), F32),
        pltpu.VMEM((planes, tok, width), BF16),
        pltpu.VMEM((planes, blocks, tok, width), BF16),
        sem((blocks - 1,)), sem((blocks - 1,)),
        sem((blocks - 1,)), sem((blocks - 1,)),
        sem((2, planes - 1)), sem((2, planes - 1)),
        sem((planes,)), sem((planes,)),
        sem((planes, chips - 1)), sem((planes, chips - 1)),
        sem((planes,)), sem((planes,)),
        sem((planes,)), sem((planes,)),
        sem((planes, chips)), sem((planes, chips)),
        sem((planes, chips)), sem((planes, chips)),
    ]
    query_grad, key_grad, weight_grad = pl.pallas_call(
        functools.partial(fused, planes, blocks),
        out_shape=(
            jax.ShapeDtypeStruct((tok, feature), BF16),
            jax.ShapeDtypeStruct((tok, feature), BF16),
            jax.ShapeDtypeStruct((rows, width), F32),
        ),
        in_specs=[vmem] * 6 + [pl.BlockSpec(memory_space=pltpu.SMEM)],
        out_specs=(vmem, vmem, vmem),
        scratch_shapes=scratch,
        compiler_params=pltpu.CompilerParams(
            collective_id=0, has_side_effects=True, vmem_limit_bytes=VMEM_LIMIT
        ),
    )(queries[0], keys[0], values[0], out_grad[0], inputs[0], log_gate[0], boundaries)
    return query_grad[None], key_grad[None], weight_grad


VMEM_LIMIT = 60 * 2**20


def per_device(mesh, inputs, queries, keys, values, out_grad, log_gate, boundaries):
    planes, blocks = mesh.shape["dp"], mesh.shape["ctx"]
    arrays = (inputs, queries, keys, values, out_grad, log_gate, boundaries)
    tok, feature = queries.shape[1:]
    gathered = 2 * planes * blocks * tok * (feature // planes + inputs.shape[2] // blocks)
    if blocks != 8 or planes < 3 or gathered + 32 * tok * feature * 2 > VMEM_LIMIT:
        return per_device_plain(*arrays)
    return per_device_fused(planes, blocks, *arrays)


def solution(mesh):
    in_specs = (
        P("dp", "ctx", None),
        P("dp", "ctx", None),
        P("dp", "ctx", None),
        P("dp", "ctx", None),
        P("dp", "ctx", None),
        P("dp", None, "ctx"),
        P("dp", None),
    )
    out_specs = (P("dp", "ctx", None), P("dp", "ctx", None), P("ctx", "dp"))
    return jax.shard_map(
        functools.partial(per_device, mesh), mesh=mesh, in_specs=in_specs, out_specs=out_specs, check_vma=False
    )
```

```python
import functools

import jax
import jax.numpy as jnp
from jax import lax
from jax.experimental import pallas as pl
from jax.experimental.pallas import tpu as pltpu
from jax.sharding import PartitionSpec as P


def head_major(array, tok_rows, head_count, head_size):
    return array[0].reshape(tok_rows, head_count, head_size).transpose(1, 0, 2)


def row_major(array, tok_rows, feature_width):
    return array.astype(jnp.bfloat16).transpose(1, 0, 2).reshape(tok_rows, feature_width)


def per_device_plain(inputs, queries, keys, values, out_grad, log_gate, boundaries):
    tok_rows = queries.shape[1]
    feature_width = queries.shape[2]
    head_count = log_gate.shape[1]
    head_size = feature_width // head_count
    query_one = head_major(queries, tok_rows, head_count, head_size)
    key_one = head_major(keys, tok_rows, head_count, head_size)
    value_one = head_major(values, tok_rows, head_count, head_size)
    grad_one = head_major(out_grad, tok_rows, head_count, head_size)
    token_one = inputs[0]
    bounds = boundaries[0]
    begin_at = lax.axis_index("ctx") * tok_rows
    positions = begin_at + jnp.arange(tok_rows, dtype=jnp.int32)
    segment_ids = jnp.sum((bounds[None, :] <= positions[:, None]).astype(jnp.int32), axis=1)
    segment_in = jnp.sum((bounds <= begin_at - 1).astype(jnp.int32))
    cumulative = jnp.cumsum(log_gate[0], axis=1)
    enter_weight = jnp.where((segment_ids == segment_in)[None, :], jnp.exp(cumulative), 0.0)
    leave_weight = jnp.where(
        (segment_ids == segment_ids[-1])[None, :], jnp.exp(cumulative[:, -1:] - cumulative), 0.0
    )
    causal = (positions[:, None] >= positions[None, :]) & (
        segment_ids[:, None] == segment_ids[None, :]
    )
    decay_table = jnp.exp(
        jnp.where(causal[None], cumulative[:, :, None] - cumulative[:, None, :], -1e30)
    )
    through = enter_weight[:, -1].astype(jnp.bfloat16)
    weighted_keys = (leave_weight[:, :, None] * key_one).astype(jnp.bfloat16)
    local_state = jnp.einsum(
        "hsd,hse->hde", weighted_keys, value_one, preferred_element_type=jnp.float32
    )
    weighted_queries = (enter_weight[:, :, None] * query_one).astype(jnp.bfloat16)
    back_state = jnp.einsum(
        "htd,hte->hde", weighted_queries, grad_one, preferred_element_type=jnp.float32
    )
    groups = lax.axis_size("ctx")
    extra = jnp.broadcast_to(through[:, None, None], (head_count, 16, head_size))
    packed = jnp.concatenate(
        [local_state.astype(jnp.bfloat16), back_state.astype(jnp.bfloat16), extra], axis=1
    )
    packed = lax.all_to_all(packed, "ctx", 0, 0, tiled=True)
    packed = packed.reshape(groups, head_count // groups, 2 * head_size + 16, head_size)
    ahead = packed[:, :, :head_size].astype(jnp.float32)
    behind = packed[:, :, head_size : 2 * head_size].astype(jnp.float32)
    factor = packed[:, :, 2 * head_size, :1, None].astype(jnp.float32)
    state_in = [jnp.zeros_like(ahead[0])]
    state_back = [jnp.zeros_like(ahead[0])]
    for block in range(groups - 1):
        state_in.append(factor[block] * state_in[-1] + ahead[block])
        late = groups - 1 - block
        state_back.append(factor[late] * state_back[-1] + behind[late])
    carried = jnp.concatenate([jnp.stack(state_in), jnp.stack(state_back[::-1])], axis=2)
    carried = carried.astype(jnp.bfloat16).reshape(head_count, 2 * head_size, head_size)
    carried = lax.all_to_all(carried, "ctx", 0, 0, tiled=True)
    carried_in, carried_back = carried[:, :head_size], carried[:, head_size:]
    score_grad = (
        decay_table
        * jnp.einsum("htd,hsd->hts", grad_one, value_one, preferred_element_type=jnp.float32)
    ).astype(jnp.bfloat16)
    score_keys = (
        decay_table
        * jnp.einsum("htd,hsd->hts", query_one, key_one, preferred_element_type=jnp.float32)
    ).astype(jnp.bfloat16)
    query_new = jnp.einsum(
        "hts,hsd->htd", score_grad, key_one, preferred_element_type=jnp.float32
    ) + enter_weight[:, :, None] * jnp.einsum(
        "hte,hde->htd", grad_one, carried_in, preferred_element_type=jnp.float32
    )
    key_new = jnp.einsum(
        "hts,htd->hsd", score_grad, query_one, preferred_element_type=jnp.float32
    ) + leave_weight[:, :, None] * jnp.einsum(
        "hse,hde->hsd", value_one, carried_back, preferred_element_type=jnp.float32
    )
    value_new = jnp.einsum(
        "hts,htd->hsd", score_keys, grad_one, preferred_element_type=jnp.float32
    ) + leave_weight[:, :, None] * jnp.einsum(
        "hsd,hde->hse", key_one, carried_back, preferred_element_type=jnp.float32
    )
    query_grad = row_major(query_new, tok_rows, feature_width).reshape(1, tok_rows, feature_width)
    key_grad = row_major(key_new, tok_rows, feature_width).reshape(1, tok_rows, feature_width)
    value_grad = row_major(value_new, tok_rows, feature_width)
    token_all = lax.all_to_all(token_one, "ctx", 1, 0, tiled=True)
    token_all = lax.all_gather(token_all, "dp")
    value_all = lax.all_to_all(value_grad, "dp", 1, 0, tiled=True)
    value_all = lax.all_gather(value_all, "ctx")
    sequences = token_all.shape[0]
    token_all = token_all.reshape(sequences, groups, tok_rows, -1).transpose(1, 0, 2, 3)
    token_all = token_all.reshape(groups * sequences * tok_rows, -1)
    value_all = value_all.reshape(groups * sequences * tok_rows, -1)
    weight_grad = lax.dot_general(
        token_all, value_all, (((0,), (0,)), ((), ())), preferred_element_type=jnp.float32
    )
    return (query_grad, key_grad, weight_grad)


F32, BF16 = jnp.float32, jnp.bfloat16


def dot(left, right, left_dim, right_dim):
    return lax.dot_general(
        left, right, (((left_dim,), (right_dim,)), ((), ())), preferred_element_type=F32
    )


def push(src, dst, send_sem, recv_sem, dp, ctx):
    return pltpu.make_async_remote_copy(
        src_ref=src,
        dst_ref=dst,
        send_sem=send_sem,
        recv_sem=recv_sem,
        device_id=(dp, ctx),
        device_id_type=pl.DeviceIdType.MESH,
    )


def fused(
    planes, blocks, q, k, v, g, x, gate, bounds, qg, kg, wg,
    cum, decay_bias, enter_bias, leave_bias, through, xt_own, xt,
    local, mate_local, chip_state, arrived, carried, mate_carried, qi, ki, vi, vsend, vall,
    t_s, t_r, xa_s, xa_r, xz_s, xz_r, m1_s, m1_r, cs_s, cs_r, m2_s, m2_r, vz_s, vz_r,
    vb_s, vb_r, vm_s, vm_r,
):
    tok, feature = q.shape
    heads = gate.shape[0]
    size = feature // heads
    chunk = heads // planes
    half = chunk // 2
    rows = xt.shape[1]
    chips = blocks // 2
    d, c = lax.axis_index("dp"), lax.axis_index("ctx")
    core, chip = lax.rem(c, 2), lax.div(c, 2)
    mate = c + 1 - 2 * core
    first = core == 0

    barrier = pltpu.get_barrier_semaphore()
    for step in range(1, blocks):
        pl.semaphore_signal(
            barrier, inc=1, device_id=(d, lax.rem(c + step, blocks)),
            device_id_type=pl.DeviceIdType.MESH,
        )
    for step in range(1, planes):
        pl.semaphore_signal(
            barrier, inc=1, device_id=(lax.rem(d + step, planes), c),
            device_id_type=pl.DeviceIdType.MESH,
        )

    for part in range(x.shape[1] // 128):
        xt_own[part * 128 : (part + 1) * 128, :] = x[:, part * 128 : (part + 1) * 128].T
    pl.semaphore_wait(barrier, blocks - 1 + planes - 1)

    def columns(block):
        return pl.ds(pl.multiple_of(block * tok, tok), tok)

    def token_push(step):
        to = lax.rem(c + step, blocks)
        return push(
            xt_own.at[pl.ds(pl.multiple_of(to * rows, rows), rows), :],
            xt.at[d, :, columns(c)], xa_s.at[step - 1], xa_r.at[step - 1], d, to,
        )

    for step in range(1, blocks):
        token_push(step).start()
    xt[d, :, columns(c)] = xt_own[pl.ds(pl.multiple_of(c * rows, rows), rows), :]

    begin = c * tok
    at_t = lax.broadcasted_iota(jnp.int32, (tok, tok), 0)
    at_s = lax.broadcasted_iota(jnp.int32, (tok, tok), 1)
    seg_t = jnp.zeros((tok, tok), jnp.int32)
    seg_s = jnp.zeros((tok, tok), jnp.int32)
    seg_in = jnp.zeros((tok, tok), jnp.int32)
    seg_last = jnp.zeros((tok, tok), jnp.int32)
    for index in range(bounds.shape[1]):
        edge = jnp.full((tok, tok), bounds[0, index] - begin, jnp.int32)
        seg_t += (edge <= at_t).astype(jnp.int32)
        seg_s += (edge <= at_s).astype(jnp.int32)
        seg_in += (edge <= -1).astype(jnp.int32)
        seg_last += (edge <= tok - 1).astype(jnp.int32)
    decay_bias[...] = jnp.where((at_t >= at_s) & (seg_t == seg_s), 0.0, -1e30)
    enter_bias[...] = jnp.where(seg_t == seg_in, 0.0, -1e30)
    leave_bias[...] = jnp.where(seg_t == seg_last, 0.0, -1e30)
    cum[...] = lax.dot_general(
        gate[...], (at_t <= at_s).astype(F32), (((1,), (0,)), ((), ())),
        precision=lax.Precision.HIGHEST, preferred_element_type=F32,
    )
    total = jnp.broadcast_to(cum[:, tok - 1 : tok], (heads, size))
    through[c] = jnp.exp(total + enter_bias[tok - 1 : tok, :]).astype(BF16).astype(F32)

    def through_push(step):
        return push(
            through.at[c], through.at[c], t_s.at[step - 1], t_r.at[step - 1],
            d, lax.rem(c + step, blocks),
        )

    for step in range(1, blocks):
        through_push(step).start()

    def head_columns(head):
        return pl.ds(pl.multiple_of(head * size, size), size)

    def weights(head):
        at_row = jnp.broadcast_to(cum[pl.ds(head, 1), :], (size, tok))
        at_col = at_row.T
        enter = jnp.exp(at_col + enter_bias[...])
        leave = jnp.exp(at_col[tok - 1 : tok, :] - at_col + leave_bias[...])
        return at_row, at_col, enter, leave

    def chunk_head(i, j):
        return lax.rem(d + i + 1, planes) * chunk + j

    def mate_push(i):
        return push(local.at[i, 1 - core], mate_local.at[i], m1_s.at[i], m1_r.at[i], d, mate)

    def halves(body):
        lax.fori_loop(0, 2, lambda part, carry: (body(part), carry)[1], 0)

    def local_chunk(i):
        def body(part):
            for j in range(half):
                head = chunk_head(i, part * half + j)
                cols = head_columns(head)
                _, _, enter, leave = weights(head)
                weighted_keys = (leave * k[:, cols].astype(F32)).astype(BF16)
                weighted_queries = (enter * q[:, cols].astype(F32)).astype(BF16)
                local[i, part, 0, j] = dot(weighted_keys, v[:, cols], 0, 0).astype(BF16)
                local[i, part, 1, j] = dot(weighted_queries, g[:, cols], 0, 0).astype(BF16)

        halves(body)
        mate_push(i).start()

    def through_wait():
        for step in range(1, blocks):
            frm = lax.rem(c - step + blocks, blocks)
            push(
                through.at[frm], through.at[frm], t_s.at[step - 1], t_r.at[step - 1], d, frm
            ).wait_recv()

    def state_push(i, step):
        ahead = chip + step
        return push(
            chip_state.at[i, lax.div(ahead, chips)], arrived.at[i, step - 1],
            cs_s.at[i, step - 1], cs_r.at[i, step - 1], d, 2 * lax.rem(ahead, chips) + core,
        )

    def chip_chunk(i):
        mate_push(i).wait_recv()
        for j in range(half):
            head = chunk_head(i, core * half + j)
            mine = through[c, pl.ds(head, 1), :]
            other = through[mate, pl.ds(head, 1), :]
            chip_state[i, 0, j] = (
                jnp.where(first, other, 1.0) * local[i, core, 0, j].astype(F32)
                + jnp.where(first, 1.0, mine) * mate_local[i, 0, j].astype(F32)
            ).astype(BF16)
            chip_state[i, 1, j] = (
                jnp.where(first, 1.0, other) * local[i, core, 1, j].astype(F32)
                + jnp.where(first, mine, 1.0) * mate_local[i, 1, j].astype(F32)
            ).astype(BF16)
        for step in range(1, chips):
            state_push(i, step).start()

    def token_wait():
        for step in range(1, blocks):
            token_push(step).wait_send()
            frm = lax.rem(c - step + blocks, blocks)
            push(
                xt.at[d, :, columns(frm)], xt.at[d, :, columns(frm)],
                xa_s.at[step - 1], xa_r.at[step - 1], d, frm,
            ).wait_recv()

    def chain(step, act):
        @pl.when((d >= step - 1) & (d + 1 < planes))
        def _():
            piece = xt.at[d - (step - 1)]
            act(push(piece, piece, xz_s.at[0, step - 1], xz_r.at[0, step - 1], d + 1, c))

        @pl.when((d + step - 1 < planes) & (d >= 1))
        def _():
            piece = xt.at[d + step - 1]
            act(push(piece, piece, xz_s.at[1, step - 1], xz_r.at[1, step - 1], d - 1, c))

    def chain_wait(step):
        @pl.when(d >= step)
        def _():
            piece = xt.at[d - step]
            push(piece, piece, xz_s.at[0, step - 1], xz_r.at[0, step - 1], d - 1, c).wait_recv()

        @pl.when(d + step < planes)
        def _():
            piece = xt.at[d + step]
            push(piece, piece, xz_s.at[1, step - 1], xz_r.at[1, step - 1], d + 1, c).wait_recv()

    def inner_chunk(i):
        def body(part):
            for j in range(half):
                head = chunk_head(i, part * half + j)
                cols = head_columns(head)
                at_row = jnp.broadcast_to(cum[pl.ds(head, 1), :], (size, tok))
                decay = jnp.exp(at_row.T - at_row + decay_bias[...])
                qh, kh, vh, gh = q[:, cols], k[:, cols], v[:, cols], g[:, cols]
                score_grad = (decay * dot(gh, vh, 1, 1)).astype(BF16)
                score_keys = (decay * dot(qh, kh, 1, 1)).astype(BF16)
                qi[:, cols] = dot(score_grad, kh, 1, 0)
                ki[:, cols] = dot(score_grad, qh, 0, 0)
                vi[:, cols] = dot(score_keys, gh, 0, 0)

        halves(body)

    def carried_push(i):
        return push(mate_carried.at[i], carried.at[i, core], m2_s.at[i], m2_r.at[i], d, mate)

    def carry_chunk(i):
        for step in range(1, chips):
            state_push(i, step).wait_recv()
        for j in range(half):
            head = chunk_head(i, core * half + j)
            mine = through[c, pl.ds(head, 1), :]
            other = through[mate, pl.ds(head, 1), :]
            sums = []
            for back in (False, True):
                state = jnp.zeros((size, size), F32)
                weight = jnp.ones((1, size), F32)
                for far in range(1, chips):
                    if back:
                        valid = chip + far < chips
                        source, slot = lax.rem(chip + far, chips), chips - far - 1
                    else:
                        valid = chip >= far
                        source, slot = lax.rem(chip - far + chips, chips), far - 1
                    state += jnp.where(valid, weight, 0.0) * arrived[i, slot, j].astype(F32)
                    weight = weight * (
                        through[2 * source, pl.ds(head, 1), :]
                        * through[2 * source + 1, pl.ds(head, 1), :]
                    )
                sums.append(state)
            came, back = sums
            late = jnp.where(first, 0.0, 1.0)
            early = 1.0 - late
            carried[i, core, 0, j] = (
                jnp.where(first, 1.0, other) * came + late * mate_local[i, 0, j].astype(F32)
            ).astype(BF16)
            carried[i, core, 1, j] = (
                jnp.where(first, other, 1.0) * back + early * mate_local[i, 1, j].astype(F32)
            ).astype(BF16)
            mate_carried[i, 0, j] = (
                jnp.where(first, mine, 1.0) * came + early * local[i, core, 0, j].astype(F32)
            ).astype(BF16)
            mate_carried[i, 1, j] = (
                jnp.where(first, 1.0, mine) * back + late * local[i, core, 1, j].astype(F32)
            ).astype(BF16)
        carried_push(i).start()

    def value_push(i):
        return push(
            vsend.at[i], vall.at[d, c], vz_s.at[i], vz_r.at[i], lax.rem(d + i + 1, planes), c
        )

    def finish(i):
        push(
            carried.at[i, 1 - core], carried.at[i, 1 - core], m2_s.at[i], m2_r.at[i], d, mate
        ).wait_recv()
        def body(part):
            for j in range(half):
                head = chunk_head(i, part * half + j)
                cols = head_columns(head)
                _, _, enter, leave = weights(head)
                came, back = carried[i, part, 0, j], carried[i, part, 1, j]
                vsend[i, :, head_columns(part * half + j)] = (
                    vi[:, cols] + leave * dot(k[:, cols], back, 1, 0)
                ).astype(BF16)
                qg[:, cols] = (qi[:, cols] + enter * dot(g[:, cols], came, 1, 1)).astype(BF16)
                kg[:, cols] = (ki[:, cols] + leave * dot(v[:, cols], back, 1, 1)).astype(BF16)

        halves(body)
        if i == planes - 1:
            vall[d, c] = vsend[i]
        else:
            value_push(i).start()

    def source_plane(i):
        return lax.rem(d - i - 1 + planes, planes)

    across = chip + 1 - 2 * lax.rem(chip, 2)
    along = lax.rem(chip + 2, chips)
    corner = chips - 1 - chip

    def spread(i, act):
        piece = vall.at[source_plane(i), c]
        for slot, to in enumerate((across, along)):
            act(push(piece, piece, vb_s.at[i, slot], vb_r.at[i, slot], d, 2 * to + core))
        act(push(piece, piece, vm_s.at[i, 0], vm_r.at[i, 0], d, mate))

    def receive(i):
        if i < planes - 1:
            piece = vall.at[source_plane(i), c]
            push(piece, piece, vz_s.at[i], vz_r.at[i], source_plane(i), c).wait_recv()
        spread(i, lambda copy: copy.start())

    def forward(i, act, wait):
        for slot, (frm, to) in enumerate(((across, along), (along, across))):
            piece = vall.at[source_plane(i), 2 * frm + core]
            if wait:
                push(
                    piece, piece, vb_s.at[i, slot], vb_r.at[i, slot], d, 2 * frm + core
                ).wait_recv()
            part = vall.at[source_plane(i), 2 * frm + core, pl.ds(slot * (tok // 2), tok // 2), :]
            act(push(part, part, vb_s.at[i, 2 + slot], vb_r.at[i, 2 + slot], d, 2 * to + core))
            act(push(piece, piece, vm_s.at[i, 1 + slot], vm_r.at[i, 1 + slot], d, mate))

    def forward_corner(i, act, wait):
        frm = 2 * corner + core
        if wait:
            for slot, via in enumerate((along, across)):
                part = vall.at[source_plane(i), frm, pl.ds(slot * (tok // 2), tok // 2), :]
                push(
                    part, part, vb_s.at[i, 2 + slot], vb_r.at[i, 2 + slot], d, 2 * via + core
                ).wait_recv()
        piece = vall.at[source_plane(i), frm]
        act(push(piece, piece, vm_s.at[i, 3], vm_r.at[i, 3], d, mate))

    def multiply(i):
        plane = source_plane(i)
        for slot, frm in enumerate((chip, across, along, corner)):
            piece = vall.at[plane, 2 * frm + 1 - core]
            push(piece, piece, vm_s.at[i, slot], vm_r.at[i, slot], d, mate).wait_recv()
        width = 256

        def tile(index, carry):
            cols = pl.ds(pl.multiple_of(index * width, width), width)
            right = vall[plane, :, :, cols].reshape(blocks * tok, width)
            product = dot(xt[plane], right, 1, 0)
            wg[:, cols] = product if i == 0 else wg[:, cols] + product
            return carry

        lax.fori_loop(0, wg.shape[1] // width, tile, 0)

    start = lambda copy: copy.start()
    last = planes - 1

    local_chunk(0)
    for i in range(1, planes + 1):
        if i < planes:
            local_chunk(i)
        if i == 1:
            through_wait()
        chip_chunk(i - 1)
        if i == min(2, planes):
            token_wait()
            chain(1, start)
    inner_chunk(0)
    carry_chunk(0)
    for i in range(planes):
        if i < last:
            inner_chunk(i + 1)
        if i == 0:
            chain_wait(1)
            chain(2, start)
        finish(i)
        if i == last - 1:
            for step in range(2, last):
                chain_wait(step)
                chain(step + 1, start)
        if i == last:
            receive(last)
        if i > 0:
            receive(i - 1)
        if i > 1:
            forward(i - 2, start, True)
        if i < last:
            carry_chunk(i + 1)
    forward_corner(0, start, True)
    forward(last - 1, start, True)
    forward(last, start, True)
    for i in range(1, planes):
        forward_corner(i, start, True)
    chain_wait(last)
    for i in range(planes):
        multiply(i)

    for step in range(1, blocks):
        through_push(step).wait_send()
    for step in range(1, planes):
        chain(step, lambda copy: copy.wait_send())
    for i in range(planes):
        mate_push(i).wait_send()
        carried_push(i).wait_send()
        for step in range(1, chips):
            state_push(i, step).wait_send()
        if i < last:
            value_push(i).wait_send()
        spread(i, lambda copy: copy.wait_send())
        forward(i, lambda copy: copy.wait_send(), False)
        forward_corner(i, lambda copy: copy.wait_send(), False)


def per_device_fused(planes, blocks, inputs, queries, keys, values, out_grad, log_gate, boundaries):
    tok, feature = queries.shape[1:]
    heads = log_gate.shape[1]
    size = feature // heads
    chunk = heads // planes
    half = chunk // 2
    chips = blocks // 2
    width = feature // planes
    rows = inputs.shape[2] // blocks
    vmem = pl.BlockSpec(memory_space=pltpu.VMEM)
    sem = pltpu.SemaphoreType.DMA
    scratch = [
        pltpu.VMEM((heads, tok), F32),
        pltpu.VMEM((tok, tok), F32),
        pltpu.VMEM((tok, tok), F32),
        pltpu.VMEM((tok, tok), F32),
        pltpu.VMEM((blocks, heads, size), F32),
        pltpu.VMEM((inputs.shape[2], tok), BF16),
        pltpu.VMEM((planes, rows, blocks * tok), BF16),
        pltpu.VMEM((planes, 2, 2, half, size, size), BF16),
        pltpu.VMEM((planes, 2, half, size, size), BF16),
        pltpu.VMEM((planes, 2, half, size, size), BF16),
        pltpu.VMEM((planes, chips - 1, half, size, size), BF16),
        pltpu.VMEM((planes, 2, 2, half, size, size), BF16),
        pltpu.VMEM((planes, 2, half, size, size), BF16),
        pltpu.VMEM((tok, feature), F32),
        pltpu.VMEM((tok, feature), F32),
        pltpu.VMEM((tok, feature), F32),
        pltpu.VMEM((planes, tok, width), BF16),
        pltpu.VMEM((planes, blocks, tok, width), BF16),
        sem((blocks - 1,)), sem((blocks - 1,)),
        sem((blocks - 1,)), sem((blocks - 1,)),
        sem((2, planes - 1)), sem((2, planes - 1)),
        sem((planes,)), sem((planes,)),
        sem((planes, chips - 1)), sem((planes, chips - 1)),
        sem((planes,)), sem((planes,)),
        sem((planes,)), sem((planes,)),
        sem((planes, chips)), sem((planes, chips)),
        sem((planes, chips)), sem((planes, chips)),
    ]
    query_grad, key_grad, weight_grad = pl.pallas_call(
        functools.partial(fused, planes, blocks),
        out_shape=(
            jax.ShapeDtypeStruct((tok, feature), BF16),
            jax.ShapeDtypeStruct((tok, feature), BF16),
            jax.ShapeDtypeStruct((rows, width), F32),
        ),
        in_specs=[vmem] * 6 + [pl.BlockSpec(memory_space=pltpu.SMEM)],
        out_specs=(vmem, vmem, vmem),
        scratch_shapes=scratch,
        compiler_params=pltpu.CompilerParams(
            collective_id=0, has_side_effects=True, vmem_limit_bytes=VMEM_LIMIT
        ),
    )(queries[0], keys[0], values[0], out_grad[0], inputs[0], log_gate[0], boundaries)
    return query_grad[None], key_grad[None], weight_grad


VMEM_LIMIT = 60 * 2**20


def per_device(mesh, inputs, queries, keys, values, out_grad, log_gate, boundaries):
    planes, blocks = mesh.shape["dp"], mesh.shape["ctx"]
    arrays = (inputs, queries, keys, values, out_grad, log_gate, boundaries)
    tok, feature = queries.shape[1:]
    gathered = 2 * planes * blocks * tok * (feature // planes + inputs.shape[2] // blocks)
    if blocks != 8 or planes < 3 or gathered + 32 * tok * feature * 2 > VMEM_LIMIT:
        return per_device_plain(*arrays)
    return per_device_fused(planes, blocks, *arrays)


def solution(mesh):
    in_specs = (
        P("dp", "ctx", None),
        P("dp", "ctx", None),
        P("dp", "ctx", None),
        P("dp", "ctx", None),
        P("dp", "ctx", None),
        P("dp", None, "ctx"),
        P("dp", None),
    )
    out_specs = (P("dp", "ctx", None), P("dp", "ctx", None), P("ctx", "dp"))
    return jax.shard_map(
        functools.partial(per_device, mesh), mesh=mesh, in_specs=in_specs, out_specs=out_specs, check_vma=False
    )
```

```python
import functools

import jax
import jax.numpy as jnp
from jax import lax
from jax.experimental import pallas as pl
from jax.experimental.pallas import tpu as pltpu
from jax.sharding import PartitionSpec as P


def head_major(array, tok_rows, head_count, head_size):
    return array[0].reshape(tok_rows, head_count, head_size).transpose(1, 0, 2)


def row_major(array, tok_rows, feature_width):
    return array.astype(jnp.bfloat16).transpose(1, 0, 2).reshape(tok_rows, feature_width)


def per_device_plain(inputs, queries, keys, values, out_grad, log_gate, boundaries):
    tok_rows = queries.shape[1]
    feature_width = queries.shape[2]
    head_count = log_gate.shape[1]
    head_size = feature_width // head_count
    query_one = head_major(queries, tok_rows, head_count, head_size)
    key_one = head_major(keys, tok_rows, head_count, head_size)
    value_one = head_major(values, tok_rows, head_count, head_size)
    grad_one = head_major(out_grad, tok_rows, head_count, head_size)
    token_one = inputs[0]
    bounds = boundaries[0]
    begin_at = lax.axis_index("ctx") * tok_rows
    positions = begin_at + jnp.arange(tok_rows, dtype=jnp.int32)
    segment_ids = jnp.sum((bounds[None, :] <= positions[:, None]).astype(jnp.int32), axis=1)
    segment_in = jnp.sum((bounds <= begin_at - 1).astype(jnp.int32))
    cumulative = jnp.cumsum(log_gate[0], axis=1)
    enter_weight = jnp.where((segment_ids == segment_in)[None, :], jnp.exp(cumulative), 0.0)
    leave_weight = jnp.where(
        (segment_ids == segment_ids[-1])[None, :], jnp.exp(cumulative[:, -1:] - cumulative), 0.0
    )
    causal = (positions[:, None] >= positions[None, :]) & (
        segment_ids[:, None] == segment_ids[None, :]
    )
    decay_table = jnp.exp(
        jnp.where(causal[None], cumulative[:, :, None] - cumulative[:, None, :], -1e30)
    )
    through = enter_weight[:, -1].astype(jnp.bfloat16)
    weighted_keys = (leave_weight[:, :, None] * key_one).astype(jnp.bfloat16)
    local_state = jnp.einsum(
        "hsd,hse->hde", weighted_keys, value_one, preferred_element_type=jnp.float32
    )
    weighted_queries = (enter_weight[:, :, None] * query_one).astype(jnp.bfloat16)
    back_state = jnp.einsum(
        "htd,hte->hde", weighted_queries, grad_one, preferred_element_type=jnp.float32
    )
    groups = lax.axis_size("ctx")
    extra = jnp.broadcast_to(through[:, None, None], (head_count, 16, head_size))
    packed = jnp.concatenate(
        [local_state.astype(jnp.bfloat16), back_state.astype(jnp.bfloat16), extra], axis=1
    )
    packed = lax.all_to_all(packed, "ctx", 0, 0, tiled=True)
    packed = packed.reshape(groups, head_count // groups, 2 * head_size + 16, head_size)
    ahead = packed[:, :, :head_size].astype(jnp.float32)
    behind = packed[:, :, head_size : 2 * head_size].astype(jnp.float32)
    factor = packed[:, :, 2 * head_size, :1, None].astype(jnp.float32)
    state_in = [jnp.zeros_like(ahead[0])]
    state_back = [jnp.zeros_like(ahead[0])]
    for block in range(groups - 1):
        state_in.append(factor[block] * state_in[-1] + ahead[block])
        late = groups - 1 - block
        state_back.append(factor[late] * state_back[-1] + behind[late])
    carried = jnp.concatenate([jnp.stack(state_in), jnp.stack(state_back[::-1])], axis=2)
    carried = carried.astype(jnp.bfloat16).reshape(head_count, 2 * head_size, head_size)
    carried = lax.all_to_all(carried, "ctx", 0, 0, tiled=True)
    carried_in, carried_back = carried[:, :head_size], carried[:, head_size:]
    score_grad = (
        decay_table
        * jnp.einsum("htd,hsd->hts", grad_one, value_one, preferred_element_type=jnp.float32)
    ).astype(jnp.bfloat16)
    score_keys = (
        decay_table
        * jnp.einsum("htd,hsd->hts", query_one, key_one, preferred_element_type=jnp.float32)
    ).astype(jnp.bfloat16)
    query_new = jnp.einsum(
        "hts,hsd->htd", score_grad, key_one, preferred_element_type=jnp.float32
    ) + enter_weight[:, :, None] * jnp.einsum(
        "hte,hde->htd", grad_one, carried_in, preferred_element_type=jnp.float32
    )
    key_new = jnp.einsum(
        "hts,htd->hsd", score_grad, query_one, preferred_element_type=jnp.float32
    ) + leave_weight[:, :, None] * jnp.einsum(
        "hse,hde->hsd", value_one, carried_back, preferred_element_type=jnp.float32
    )
    value_new = jnp.einsum(
        "hts,htd->hsd", score_keys, grad_one, preferred_element_type=jnp.float32
    ) + leave_weight[:, :, None] * jnp.einsum(
        "hsd,hde->hse", key_one, carried_back, preferred_element_type=jnp.float32
    )
    query_grad = row_major(query_new, tok_rows, feature_width).reshape(1, tok_rows, feature_width)
    key_grad = row_major(key_new, tok_rows, feature_width).reshape(1, tok_rows, feature_width)
    value_grad = row_major(value_new, tok_rows, feature_width)
    token_all = lax.all_to_all(token_one, "ctx", 1, 0, tiled=True)
    token_all = lax.all_gather(token_all, "dp")
    value_all = lax.all_to_all(value_grad, "dp", 1, 0, tiled=True)
    value_all = lax.all_gather(value_all, "ctx")
    sequences = token_all.shape[0]
    token_all = token_all.reshape(sequences, groups, tok_rows, -1).transpose(1, 0, 2, 3)
    token_all = token_all.reshape(groups * sequences * tok_rows, -1)
    value_all = value_all.reshape(groups * sequences * tok_rows, -1)
    weight_grad = lax.dot_general(
        token_all, value_all, (((0,), (0,)), ((), ())), preferred_element_type=jnp.float32
    )
    return (query_grad, key_grad, weight_grad)


F32, BF16 = jnp.float32, jnp.bfloat16


def dot(left, right, left_dim, right_dim):
    return lax.dot_general(
        left, right, (((left_dim,), (right_dim,)), ((), ())), preferred_element_type=F32
    )


def push(src, dst, send_sem, recv_sem, dp, ctx):
    return pltpu.make_async_remote_copy(
        src_ref=src,
        dst_ref=dst,
        send_sem=send_sem,
        recv_sem=recv_sem,
        device_id=(dp, ctx),
        device_id_type=pl.DeviceIdType.MESH,
    )


def fused(
    planes, blocks, q_in, k_in, v_in, g_in, x_in, gate, bounds, qg_out, kg_out, wg,
    q, k, v, g, x, qg, kg, acc, io_sem,
    cum, decay_bias, enter_bias, leave_bias, through, xt_own, xt,
    local, mate_local, chip_state, arrived, carried, mate_carried, qi, ki, vi, vsend, vall,
    t_s, t_r, xa_s, xa_r, xz_s, xz_r, m1_s, m1_r, cs_s, cs_r, m2_s, m2_r, vz_s, vz_r,
    vb_s, vb_r, vm_s, vm_r,
):
    tok, feature = q.shape
    heads = gate.shape[0]
    size = feature // heads
    chunk = heads // planes
    half = chunk // 2
    rows = xt.shape[1]
    chips = blocks // 2
    d, c = lax.axis_index("dp"), lax.axis_index("ctx")
    core, chip = lax.rem(c, 2), lax.div(c, 2)
    mate = c + 1 - 2 * core
    first = core == 0

    barrier = pltpu.get_barrier_semaphore()
    for step in range(1, blocks):
        pl.semaphore_signal(
            barrier, inc=1, device_id=(d, lax.rem(c + step, blocks)),
            device_id_type=pl.DeviceIdType.MESH,
        )
    for step in range(1, planes):
        pl.semaphore_signal(
            barrier, inc=1, device_id=(lax.rem(d + step, planes), c),
            device_id_type=pl.DeviceIdType.MESH,
        )

    loads = [
        pltpu.make_async_copy(src, dst, io_sem.at[index])
        for index, (src, dst) in enumerate(
            ((x_in, x), (k_in, k), (q_in, q), (v_in, v), (g_in, g))
        )
    ]
    for load in loads:
        load.start()
    loads[0].wait()
    for part in range(x.shape[1] // 128):
        xt_own[part * 128 : (part + 1) * 128, :] = x[:, part * 128 : (part + 1) * 128].T
    pl.semaphore_wait(barrier, blocks - 1 + planes - 1)

    def columns(block):
        return pl.ds(pl.multiple_of(block * tok, tok), tok)

    def token_push(step):
        to = lax.rem(c + step, blocks)
        return push(
            xt_own.at[pl.ds(pl.multiple_of(to * rows, rows), rows), :],
            xt.at[d, :, columns(c)], xa_s.at[step - 1], xa_r.at[step - 1], d, to,
        )

    for step in range(1, blocks):
        token_push(step).start()
    xt[d, :, columns(c)] = xt_own[pl.ds(pl.multiple_of(c * rows, rows), rows), :]

    begin = c * tok
    at_t = lax.broadcasted_iota(jnp.int32, (tok, tok), 0)
    at_s = lax.broadcasted_iota(jnp.int32, (tok, tok), 1)
    seg_t = jnp.zeros((tok, tok), jnp.int32)
    seg_s = jnp.zeros((tok, tok), jnp.int32)
    seg_in = jnp.zeros((tok, tok), jnp.int32)
    seg_last = jnp.zeros((tok, tok), jnp.int32)
    for index in range(bounds.shape[1]):
        edge = jnp.full((tok, tok), bounds[0, index] - begin, jnp.int32)
        seg_t += (edge <= at_t).astype(jnp.int32)
        seg_s += (edge <= at_s).astype(jnp.int32)
        seg_in += (edge <= -1).astype(jnp.int32)
        seg_last += (edge <= tok - 1).astype(jnp.int32)
    decay_bias[...] = jnp.where((at_t >= at_s) & (seg_t == seg_s), 0.0, -1e30)
    enter_bias[...] = jnp.where(seg_t == seg_in, 0.0, -1e30)
    leave_bias[...] = jnp.where(seg_t == seg_last, 0.0, -1e30)
    cum[...] = lax.dot_general(
        gate[...], (at_t <= at_s).astype(F32), (((1,), (0,)), ((), ())),
        precision=lax.Precision.HIGHEST, preferred_element_type=F32,
    )
    total = jnp.broadcast_to(cum[:, tok - 1 : tok], (heads, size))
    through[c] = jnp.exp(total + enter_bias[tok - 1 : tok, :]).astype(BF16).astype(F32)

    def through_push(step):
        return push(
            through.at[c], through.at[c], t_s.at[step - 1], t_r.at[step - 1],
            d, lax.rem(c + step, blocks),
        )

    for step in range(1, blocks):
        through_push(step).start()

    def head_columns(head):
        return pl.ds(pl.multiple_of(head * size, size), size)

    def weights(head):
        at_row = jnp.broadcast_to(cum[pl.ds(head, 1), :], (size, tok))
        at_col = at_row.T
        enter = jnp.exp(at_col + enter_bias[...])
        leave = jnp.exp(at_col[tok - 1 : tok, :] - at_col + leave_bias[...])
        return at_row, at_col, enter, leave

    def chunk_head(i, j):
        return lax.rem(d + i, planes) * chunk + j

    def mate_push(i):
        return push(local.at[i, 1 - core], mate_local.at[i], m1_s.at[i], m1_r.at[i], d, mate)

    def halves(body):
        lax.fori_loop(0, 2, lambda part, carry: (body(part), carry)[1], 0)

    def local_chunk(i):
        def body(part):
            for j in range(half):
                head = chunk_head(i, part * half + j)
                cols = head_columns(head)
                _, _, enter, leave = weights(head)
                weighted_keys = (leave * k[:, cols].astype(F32)).astype(BF16)
                weighted_queries = (enter * q[:, cols].astype(F32)).astype(BF16)
                local[i, part, 0, j] = dot(weighted_keys, v[:, cols], 0, 0).astype(BF16)
                local[i, part, 1, j] = dot(weighted_queries, g[:, cols], 0, 0).astype(BF16)

        halves(body)
        mate_push(i).start()

    def through_wait():
        for step in range(1, blocks):
            frm = lax.rem(c - step + blocks, blocks)
            push(
                through.at[frm], through.at[frm], t_s.at[step - 1], t_r.at[step - 1], d, frm
            ).wait_recv()

    def state_push(i, step):
        ahead = chip + step
        return push(
            chip_state.at[i, lax.div(ahead, chips)], arrived.at[i, step - 1],
            cs_s.at[i, step - 1], cs_r.at[i, step - 1], d, 2 * lax.rem(ahead, chips) + core,
        )

    def chip_chunk(i):
        mate_push(i).wait_recv()
        for j in range(half):
            head = chunk_head(i, core * half + j)
            mine = through[c, pl.ds(head, 1), :]
            other = through[mate, pl.ds(head, 1), :]
            chip_state[i, 0, j] = (
                jnp.where(first, other, 1.0) * local[i, core, 0, j].astype(F32)
                + jnp.where(first, 1.0, mine) * mate_local[i, 0, j].astype(F32)
            ).astype(BF16)
            chip_state[i, 1, j] = (
                jnp.where(first, 1.0, other) * local[i, core, 1, j].astype(F32)
                + jnp.where(first, mine, 1.0) * mate_local[i, 1, j].astype(F32)
            ).astype(BF16)
        for step in range(1, chips):
            state_push(i, step).start()

    def token_wait():
        for step in range(1, blocks):
            token_push(step).wait_send()
            frm = lax.rem(c - step + blocks, blocks)
            push(
                xt.at[d, :, columns(frm)], xt.at[d, :, columns(frm)],
                xa_s.at[step - 1], xa_r.at[step - 1], d, frm,
            ).wait_recv()

    def chain(step, act):
        @pl.when((d >= step - 1) & (d + 1 < planes))
        def _():
            piece = xt.at[d - (step - 1)]
            act(push(piece, piece, xz_s.at[0, step - 1], xz_r.at[0, step - 1], d + 1, c))

        @pl.when((d + step - 1 < planes) & (d >= 1))
        def _():
            piece = xt.at[d + step - 1]
            act(push(piece, piece, xz_s.at[1, step - 1], xz_r.at[1, step - 1], d - 1, c))

    def chain_wait(step):
        @pl.when(d >= step)
        def _():
            piece = xt.at[d - step]
            push(piece, piece, xz_s.at[0, step - 1], xz_r.at[0, step - 1], d - 1, c).wait_recv()

        @pl.when(d + step < planes)
        def _():
            piece = xt.at[d + step]
            push(piece, piece, xz_s.at[1, step - 1], xz_r.at[1, step - 1], d + 1, c).wait_recv()

    def inner_chunk(i):
        def body(part):
            for j in range(half):
                head = chunk_head(i, part * half + j)
                cols = head_columns(head)
                at_row = jnp.broadcast_to(cum[pl.ds(head, 1), :], (size, tok))
                decay = jnp.exp(at_row.T - at_row + decay_bias[...])
                qh, kh, vh, gh = q[:, cols], k[:, cols], v[:, cols], g[:, cols]
                score_grad = (decay * dot(gh, vh, 1, 1)).astype(BF16)
                score_keys = (decay * dot(qh, kh, 1, 1)).astype(BF16)
                qi[:, cols] = dot(score_grad, kh, 1, 0)
                ki[:, cols] = dot(score_grad, qh, 0, 0)
                vi[:, cols] = dot(score_keys, gh, 0, 0)

        halves(body)

    def carried_push(i):
        return push(mate_carried.at[i], carried.at[i, core], m2_s.at[i], m2_r.at[i], d, mate)

    def carry_chunk(i):
        for step in range(1, chips):
            state_push(i, step).wait_recv()
        for j in range(half):
            head = chunk_head(i, core * half + j)
            mine = through[c, pl.ds(head, 1), :]
            other = through[mate, pl.ds(head, 1), :]
            sums = []
            for back in (False, True):
                state = jnp.zeros((size, size), F32)
                weight = jnp.ones((1, size), F32)
                for far in range(1, chips):
                    if back:
                        valid = chip + far < chips
                        source, slot = lax.rem(chip + far, chips), chips - far - 1
                    else:
                        valid = chip >= far
                        source, slot = lax.rem(chip - far + chips, chips), far - 1
                    state += jnp.where(valid, weight, 0.0) * arrived[i, slot, j].astype(F32)
                    weight = weight * (
                        through[2 * source, pl.ds(head, 1), :]
                        * through[2 * source + 1, pl.ds(head, 1), :]
                    )
                sums.append(state)
            came, back = sums
            late = jnp.where(first, 0.0, 1.0)
            early = 1.0 - late
            carried[i, core, 0, j] = (
                jnp.where(first, 1.0, other) * came + late * mate_local[i, 0, j].astype(F32)
            ).astype(BF16)
            carried[i, core, 1, j] = (
                jnp.where(first, other, 1.0) * back + early * mate_local[i, 1, j].astype(F32)
            ).astype(BF16)
            mate_carried[i, 0, j] = (
                jnp.where(first, mine, 1.0) * came + early * local[i, core, 0, j].astype(F32)
            ).astype(BF16)
            mate_carried[i, 1, j] = (
                jnp.where(first, 1.0, mine) * back + late * local[i, core, 1, j].astype(F32)
            ).astype(BF16)
        carried_push(i).start()

    def value_push(i):
        return push(
            vsend.at[i], vall.at[d, c], vz_s.at[i], vz_r.at[i], lax.rem(d + i, planes), c
        )

    def finish(i):
        push(
            carried.at[i, 1 - core], carried.at[i, 1 - core], m2_s.at[i], m2_r.at[i], d, mate
        ).wait_recv()
        def body(part):
            for j in range(half):
                head = chunk_head(i, part * half + j)
                cols = head_columns(head)
                _, _, enter, leave = weights(head)
                came, back = carried[i, part, 0, j], carried[i, part, 1, j]
                vsend[i, :, head_columns(part * half + j)] = (
                    vi[:, cols] + leave * dot(k[:, cols], back, 1, 0)
                ).astype(BF16)
                qg[:, cols] = (qi[:, cols] + enter * dot(g[:, cols], came, 1, 1)).astype(BF16)
                kg[:, cols] = (ki[:, cols] + leave * dot(v[:, cols], back, 1, 1)).astype(BF16)

        halves(body)
        if i == 0:
            vall[d, c] = vsend[0]
        else:
            value_push(i).start()

    def source_plane(i):
        return lax.rem(d - i + planes, planes)

    across = chip + 1 - 2 * lax.rem(chip, 2)
    along = lax.rem(chip + 2, chips)
    corner = chips - 1 - chip

    def spread(i, act):
        piece = vall.at[source_plane(i), c]
        for slot, to in enumerate((across, along)):
            act(push(piece, piece, vb_s.at[i, slot], vb_r.at[i, slot], d, 2 * to + core))
        act(push(piece, piece, vm_s.at[i, 0], vm_r.at[i, 0], d, mate))

    def receive(i):
        if i:
            piece = vall.at[source_plane(i), c]
            push(piece, piece, vz_s.at[i], vz_r.at[i], source_plane(i), c).wait_recv()
        spread(i, lambda copy: copy.start())

    def forward(i, act, wait):
        for slot, (frm, to) in enumerate(((across, along), (along, across))):
            piece = vall.at[source_plane(i), 2 * frm + core]
            if wait:
                push(
                    piece, piece, vb_s.at[i, slot], vb_r.at[i, slot], d, 2 * frm + core
                ).wait_recv()
            part = vall.at[source_plane(i), 2 * frm + core, pl.ds(slot * (tok // 2), tok // 2), :]
            act(push(part, part, vb_s.at[i, 2 + slot], vb_r.at[i, 2 + slot], d, 2 * to + core))
            act(push(piece, piece, vm_s.at[i, 1 + slot], vm_r.at[i, 1 + slot], d, mate))

    def forward_corner(i, act, wait):
        frm = 2 * corner + core
        if wait:
            for slot, via in enumerate((along, across)):
                part = vall.at[source_plane(i), frm, pl.ds(slot * (tok // 2), tok // 2), :]
                push(
                    part, part, vb_s.at[i, 2 + slot], vb_r.at[i, 2 + slot], d, 2 * via + core
                ).wait_recv()
        piece = vall.at[source_plane(i), frm]
        act(push(piece, piece, vm_s.at[i, 3], vm_r.at[i, 3], d, mate))

    def multiply(i):
        plane = source_plane(i)
        for slot, frm in enumerate((chip, across, along, corner)):
            piece = vall.at[plane, 2 * frm + 1 - core]
            push(piece, piece, vm_s.at[i, slot], vm_r.at[i, slot], d, mate).wait_recv()
        width = 256

        def tile(index, carry):
            cols = pl.ds(pl.multiple_of(index * width, width), width)
            right = vall[plane, :, :, cols].reshape(blocks * tok, width)
            product = dot(xt[plane], right, 1, 0)
            if i:
                product = acc[:, cols] + product
            if i == planes - 1:
                wg[:, cols] = product.astype(BF16)
            else:
                acc[:, cols] = product
            return carry

        lax.fori_loop(0, acc.shape[1] // width, tile, 0)

    start = lambda copy: copy.start()
    last = planes - 1

    for load in loads[1:]:
        load.wait()

    local_chunk(0)
    for i in range(1, planes + 1):
        if i < planes:
            local_chunk(i)
        if i == 1:
            through_wait()
        chip_chunk(i - 1)
        if i == min(2, planes):
            token_wait()
            chain(1, start)
    inner_chunk(0)
    carry_chunk(0)
    for i in range(planes):
        if i < last:
            inner_chunk(i + 1)
        if i == 0:
            chain_wait(1)
            chain(2, start)
        finish(i)
        if i == 0:
            receive(0)
        elif i == 1:
            forward(0, start, True)
        else:
            if i == last:
                for step in range(2, last):
                    chain_wait(step)
                    chain(step + 1, start)
            receive(i - 1)
            if i == 2:
                forward_corner(0, start, True)
            else:
                forward(i - 2, start, True)
        if i < last:
            carry_chunk(i + 1)
    stores = [
        pltpu.make_async_copy(src, dst, io_sem.at[5 + index])
        for index, (src, dst) in enumerate(((qg, qg_out), (kg, kg_out)))
    ]
    for store in stores:
        store.start()
    receive(last)
    forward(last - 1, start, True)
    for i in range(1, last):
        forward_corner(i, start, True)
    multiply(0)
    forward(last, start, True)
    for i in range(2, last):
        multiply(i)
    forward_corner(last, start, True)
    chain_wait(last)
    multiply(1)
    multiply(last)
    for store in stores:
        store.wait()

    for step in range(1, blocks):
        through_push(step).wait_send()
    for step in range(1, planes):
        chain(step, lambda copy: copy.wait_send())
    for i in range(planes):
        mate_push(i).wait_send()
        carried_push(i).wait_send()
        for step in range(1, chips):
            state_push(i, step).wait_send()
        if i:
            value_push(i).wait_send()
        spread(i, lambda copy: copy.wait_send())
        forward(i, lambda copy: copy.wait_send(), False)
        forward_corner(i, lambda copy: copy.wait_send(), False)


def per_device_fused(planes, blocks, inputs, queries, keys, values, out_grad, log_gate, boundaries):
    tok, feature = queries.shape[1:]
    heads = log_gate.shape[1]
    size = feature // heads
    chunk = heads // planes
    half = chunk // 2
    chips = blocks // 2
    width = feature // planes
    rows = inputs.shape[2] // blocks
    vmem = pl.BlockSpec(memory_space=pltpu.VMEM)
    hbm = pl.BlockSpec(memory_space=pl.ANY)
    sem = pltpu.SemaphoreType.DMA
    scratch = [
        pltpu.VMEM((tok, feature), BF16),
        pltpu.VMEM((tok, feature), BF16),
        pltpu.VMEM((tok, feature), BF16),
        pltpu.VMEM((tok, feature), BF16),
        pltpu.VMEM((tok, inputs.shape[2]), BF16),
        pltpu.VMEM((tok, feature), BF16),
        pltpu.VMEM((tok, feature), BF16),
        pltpu.VMEM((rows, width), F32),
        sem((7,)),
        pltpu.VMEM((heads, tok), F32),
        pltpu.VMEM((tok, tok), F32),
        pltpu.VMEM((tok, tok), F32),
        pltpu.VMEM((tok, tok), F32),
        pltpu.VMEM((blocks, heads, size), F32),
        pltpu.VMEM((inputs.shape[2], tok), BF16),
        pltpu.VMEM((planes, rows, blocks * tok), BF16),
        pltpu.VMEM((planes, 2, 2, half, size, size), BF16),
        pltpu.VMEM((planes, 2, half, size, size), BF16),
        pltpu.VMEM((planes, 2, half, size, size), BF16),
        pltpu.VMEM((planes, chips - 1, half, size, size), BF16),
        pltpu.VMEM((planes, 2, 2, half, size, size), BF16),
        pltpu.VMEM((planes, 2, half, size, size), BF16),
        pltpu.VMEM((tok, feature), F32),
        pltpu.VMEM((tok, feature), F32),
        pltpu.VMEM((tok, feature), F32),
        pltpu.VMEM((planes, tok, width), BF16),
        pltpu.VMEM((planes, blocks, tok, width), BF16),
        sem((blocks - 1,)), sem((blocks - 1,)),
        sem((blocks - 1,)), sem((blocks - 1,)),
        sem((2, planes - 1)), sem((2, planes - 1)),
        sem((planes,)), sem((planes,)),
        sem((planes, chips - 1)), sem((planes, chips - 1)),
        sem((planes,)), sem((planes,)),
        sem((planes,)), sem((planes,)),
        sem((planes, chips)), sem((planes, chips)),
        sem((planes, chips)), sem((planes, chips)),
    ]
    query_grad, key_grad, weight_grad = pl.pallas_call(
        functools.partial(fused, planes, blocks),
        out_shape=(
            jax.ShapeDtypeStruct((tok, feature), BF16),
            jax.ShapeDtypeStruct((tok, feature), BF16),
            jax.ShapeDtypeStruct((rows, width), BF16),
        ),
        in_specs=[hbm] * 5 + [vmem] + [pl.BlockSpec(memory_space=pltpu.SMEM)],
        out_specs=(hbm, hbm, vmem),
        scratch_shapes=scratch,
        compiler_params=pltpu.CompilerParams(
            collective_id=0, has_side_effects=True, vmem_limit_bytes=VMEM_LIMIT
        ),
    )(queries[0], keys[0], values[0], out_grad[0], inputs[0], log_gate[0], boundaries)
    return query_grad[None], key_grad[None], weight_grad.astype(F32)


VMEM_LIMIT = 60 * 2**20


def per_device(mesh, inputs, queries, keys, values, out_grad, log_gate, boundaries):
    planes, blocks = mesh.shape["dp"], mesh.shape["ctx"]
    arrays = (inputs, queries, keys, values, out_grad, log_gate, boundaries)
    tok, feature = queries.shape[1:]
    gathered = 2 * planes * blocks * tok * (feature // planes + inputs.shape[2] // blocks)
    if blocks != 8 or planes < 4 or gathered + 32 * tok * feature * 2 > VMEM_LIMIT:
        return per_device_plain(*arrays)
    return per_device_fused(planes, blocks, *arrays)


def solution(mesh):
    in_specs = (
        P("dp", "ctx", None),
        P("dp", "ctx", None),
        P("dp", "ctx", None),
        P("dp", "ctx", None),
        P("dp", "ctx", None),
        P("dp", None, "ctx"),
        P("dp", None),
    )
    out_specs = (P("dp", "ctx", None), P("dp", "ctx", None), P("ctx", "dp"))
    return jax.shard_map(
        functools.partial(per_device, mesh), mesh=mesh, in_specs=in_specs, out_specs=out_specs, check_vma=False
    )
```
